256 devices in a mesh: frame: 16 (over x_hi, y, core), row: 16 (over x_lo, z).
Axes of the slice: x: 4 (x_hi: 2, x_lo: 2; x = x_hi * 2 + x_lo), y: 4, z: 8, core: 2. Of those that a mesh axis runs over, the one named last changes fastest.
Arguments:
- proj: bfloat16 [16, 2048, 12288], P('frame', 'row'), may hold values from -6 to 6
- dout: bfloat16 [16, 2048, 4096], P('frame', 'row'), may hold values from -6 to 6
- filt: float32 [4096, 2048], P('row'), may hold values from -0.125 to 0.125
- out_weight: bfloat16 [4096, 4096], P('row', 'frame'), may hold values from -0.09375 to 0.09375
Outputs:
- grad_proj: bfloat16 [16, 2048, 12288], P('frame', 'row')
- grad_out_weight: float32 [4096, 4096], P('row', 'frame')
- grad_filter: float32 [4096, 2048], P('row', 'frame')
The draws below stay inside these ranges and needn't reach their ends.
All inputs are finite; a program needn't handle non-finite values.
Results may differ from the reference program's by a relative error of at most 0.0049.
Values may be sent and summed in bfloat16 or wider, within the bound.
A program may use at most 128 MiB of HBM per device.

```python
import jax
import jax.numpy as jnp
from jax import lax

D = 4096
LR = 64
LC = 32
FRAMES = 16
PROJ = 12288


def raised(result, own_key, source, target, blocks, factor):
    def block_of(dim):
        return (jnp.arange(result.shape[dim]) // (result.shape[dim] // blocks)).reshape((-1,) + (1,) * (result.ndim - 1 - dim))

    near = jax.random.permutation(own_key, blocks)[block_of(target)]
    second = (block_of(target) + blocks // 2) % blocks
    return jnp.where((block_of(source) == near) | (block_of(source) == second), factor * result, result)


def block_levels(rng, shape, pieces, least, top_value):
    loudness = 1.0
    for position, blocks in pieces:
        steps = jax.random.uniform(jax.random.fold_in(jax.random.fold_in(rng, 6), position), (blocks,), jnp.float32, least / len(pieces), top_value / len(pieces))
        loudness = loudness * jnp.repeat(jnp.exp(steps), shape[position] // blocks).reshape((-1,) + (1,) * (len(shape) - 1 - position))
    return loudness


def centred(stream_key, shape, spread, limit, split=(), kind=jnp.bfloat16):
    result = spread * jax.random.normal(stream_key, shape, jnp.float32)
    if split:
        result = result * block_levels(stream_key, shape, split, -0.22, 0.18)
    return jnp.clip(result, -limit, limit).astype(kind)


def heavy_noise(stream_key, dims, spread, most, pieces, heavy, dtype=jnp.bfloat16):
    result = spread * jax.random.normal(stream_key, dims, jnp.float32)
    if pieces:
        result = result * block_levels(stream_key, dims, pieces, -0.22, 0.18)
    return jnp.clip(raised(result, jax.random.fold_in(stream_key, 3), *heavy), -most, most).astype(dtype)


def setup_inputs(seed: int = 0) -> dict:
    key_of = jax.random.split(jax.random.key(seed), 5)
    proj = centred(key_of[0], (FRAMES, LR * LC, PROJ), 1.0, 6.0, ((0, 16), (1, 16)))
    dout = heavy_noise(key_of[1], (FRAMES, LR * LC, D), 1.0, 6.0, ((0, 16), (1, 16)), (0, 2, 16, 2.0))
    filt = centred(key_of[2], (D, LR * LC), (LR * LC) ** -0.5, 0.125, ((0, 16),), jnp.float32)
    out_weight = centred(key_of[3], (D, D), D ** -0.5, 0.09375, ((0, 16), (1, 16)))
    return dict(proj=proj, dout=dout, filt=filt, out_weight=out_weight)


def reference(proj, dout, filt, out_weight):
    width = out_weight.shape[0]
    spectrum = jnp.fft.fft2(filt.reshape(width, LR, LC), axes=(1, 2))
    spectrum = jnp.transpose(spectrum, (1, 2, 0))
    frames = proj.shape[0]

    def one_frame(carry, inputs):
        grad_weight, acc_re, acc_im = carry
        frame_proj, frame_dout = inputs
        value = frame_proj[:, :width].astype(jnp.float32)
        gate_a = frame_proj[:, width:2 * width].astype(jnp.float32)
        gate_b = frame_proj[:, 2 * width:].astype(jnp.float32)
        mixed = (gate_a * value).astype(jnp.bfloat16)
        plane = mixed.astype(jnp.float32).reshape(LR, LC, width)
        mixed_hat = jnp.fft.fft2(plane, axes=(0, 1))
        conv = jnp.real(jnp.fft.ifft2(mixed_hat * spectrum, axes=(0, 1))).reshape(LR * LC, width)
        gated = (gate_b * conv).astype(jnp.bfloat16)
        dgated = jnp.dot(frame_dout, out_weight.T, preferred_element_type=jnp.float32)
        grad_weight = grad_weight + jnp.dot(gated.T, frame_dout, preferred_element_type=jnp.float32)
        dconv = dgated * gate_b
        dconv_hat = jnp.fft.fft2(dconv.reshape(LR, LC, width), axes=(0, 1))
        dmixed = jnp.real(jnp.fft.ifft2(dconv_hat * jnp.conj(spectrum), axes=(0, 1)))
        dmixed = dmixed.reshape(LR * LC, width).astype(jnp.bfloat16).astype(jnp.float32)
        cross = dconv_hat * jnp.conj(mixed_hat)
        acc_re = acc_re + jnp.real(cross)
        acc_im = acc_im + jnp.imag(cross)
        dgate_b = (dgated * conv).astype(jnp.bfloat16)
        grads = jnp.concatenate([(dmixed * gate_a).astype(jnp.bfloat16), (dmixed * value).astype(jnp.bfloat16), dgate_b], axis=1)
        return (grad_weight, acc_re, acc_im), grads

    start = (jnp.zeros((width, width), jnp.float32), jnp.zeros((LR, LC, width), jnp.float32), jnp.zeros((LR, LC, width), jnp.float32))
    (grad_weight, acc_re, acc_im), grad_proj = lax.scan(one_frame, start, (proj, dout))
    grad_filter = jnp.real(jnp.fft.ifft2(acc_re + 1j * acc_im, axes=(0, 1)))
    grad_filter = jnp.transpose(grad_filter, (2, 0, 1)).reshape(width, LR * LC)
    return grad_proj, grad_weight / frames, grad_filter / frames
```

```python
import functools

import jax
import jax.numpy as jnp
import ml_dtypes
import numpy as np
from jax import lax
from jax.experimental import pallas as pl
from jax.experimental.pallas import tpu as pltpu
from jax.sharding import PartitionSpec as P

LR = 64
LC = 32
POS = LR * LC
HALF = POS // 2
G = 8
MESH = pl.DeviceIdType.MESH
BF = jnp.bfloat16
F32 = jnp.float32


def split_table(table):
    high = table.astype(ml_dtypes.bfloat16)
    low = (table - high.astype(np.float64)).astype(ml_dtypes.bfloat16)
    return high, low


def build_tables():
    j = np.arange(LC)
    fwd = np.zeros((LC, LC))
    inv = np.zeros((LC, LC))
    fwd[0], inv[:, 0] = 1.0, 1.0
    fwd[1] = np.cos(np.pi * j)
    inv[:, 1] = np.cos(np.pi * j)
    for l in range(1, LC // 2):
        angle = 2 * np.pi * ((j * l) % LC) / LC
        fwd[2 * l], fwd[2 * l + 1] = np.cos(angle), -np.sin(angle)
        inv[:, 2 * l], inv[:, 2 * l + 1] = 2 * np.cos(angle), -2 * np.sin(angle)
    inv = inv / POS
    eye = np.eye(G)
    col_fwd = np.einsum("qj,ab->qabj", fwd, eye).reshape(G * LC, G * LC)
    col_inv = np.einsum("jq,ab->ajqb", inv, eye).reshape(G * LC, G * LC)
    i = np.arange(LR)
    angle = 2 * np.pi * ((i[:, None] * i[None, :]) % LR) / LR
    c, s = np.cos(angle), np.sin(angle)
    o = np.zeros_like(c)
    row_fwd = np.block([[c, s], [-s, c]])
    row_inv = np.block([[c, -s], [s, c]])
    edge_fwd = np.block([[c, o], [-s, o], [o, c], [o, -s]])
    edge_inv = np.block([[c, -s, o, o], [o, o, c, -s]])
    out = []
    for table in (col_fwd, row_fwd, edge_fwd, row_inv, edge_inv, col_inv):
        out.extend(split_table(table))
    return tuple(out)


def split(x):
    high = x.astype(BF)
    return high, (x - high.astype(F32)).astype(BF)


def dot(a, b):
    return jnp.dot(a, b, preferred_element_type=F32)


def dot_t(a, b):
    return lax.dot_general(a, b, (((1,), (1,)), ((), ())), preferred_element_type=F32)


def dot3(high, low, x, product=dot):
    x_high, x_low = split(x)
    return product(high, x_high) + product(high, x_low) + product(low, x_high)


def kernel(
    R, F, D,
    proj, dout, w, filt,
    a1h, a1l, a2h, a2l, azh, azl, b2h, b2l, bzh, bzl, b1h, b1l,
    out, gw_out, gf_out,
    value, gate_a, mx, mch, gmn, cmn, cvo, dh, w2, fsp, msp, dsp, tmp, gt, dcv, dch, dg, dms, dmt, gws, gwr, gfs, gfr,
    local, ring_s, ring_r, mx_s, mx_r, gate_s, gate_r, w_s, w_r, x_s, x_r, dg_s, dg_r, dm_s, dm_r, gw_s, gw_r, gf_s, gf_r,
):
    NZ = R // 2
    TB, CB, DB, PB = POS // R, D // R, D // F, POS // F
    f, r = lax.axis_index("frame"), lax.axis_index("row")
    xl, z = lax.div(r, NZ), lax.rem(r, NZ)
    pr = (1 - xl) * NZ + z
    right = xl * NZ + lax.rem(z + 1, NZ)
    left = xl * NZ + lax.rem(z + NZ - 1, NZ)

    def at(index, size):
        return pl.ds(pl.multiple_of(index * size, size), size)

    def remote(src, dst, send, recv, frame, row):
        return pltpu.make_async_remote_copy(
            src_ref=src, dst_ref=dst, send_sem=send, recv_sem=recv,
            device_id={"frame": frame, "row": row}, device_id_type=MESH,
        )

    def loop(start, stop, step):
        def body(k, carry):
            step(k)
            return carry

        lax.fori_loop(start, stop, body, 0)

    own_dout = pltpu.make_async_copy(dout, dh.at[at(z, TB), :], local.at[0])
    own_w = pltpu.make_async_copy(w, w2.at[pl.ds(0, CB), at(f, DB)], local.at[1])
    own_gate = [
        pltpu.make_async_copy(proj.at[:, at(2 * R + c, CB)], gmn.at[n, at(z, TB), :], local.at[2 + n])
        for n, c in enumerate((r, pr))
    ]
    own_value = pltpu.make_async_copy(proj.at[:, pl.ds(0, D)], value, local.at[8])
    own_a = pltpu.make_async_copy(proj.at[:, pl.ds(D, D)], gate_a, local.at[9])
    own_value.start()
    own_a.start()
    own_dout.start()
    own_w.start()
    for copy in own_gate:
        copy.start()

    barrier = pltpu.get_barrier_semaphore()

    def greet(frame, row):
        pl.semaphore_signal(barrier, inc=1, device_id={"frame": frame, "row": row}, device_id_type=MESH)

    loop(1, R, lambda k: greet(f, lax.rem(r + k, R)))

    def greet_plane(k):
        greet(lax.rem(f + k, F), r)
        greet(lax.rem(f + k, F), pr)

    loop(1, F, greet_plane)

    own_value.wait()
    own_a.wait()
    mx[...] = (value[...].astype(F32) * gate_a[...].astype(F32)).astype(BF)
    own_mx = pltpu.make_async_copy(mx.at[:, at(r, CB)], mch.at[at(r, TB), :], local.at[4])
    own_mx.start()
    own_dout.wait()
    pl.semaphore_wait(barrier, (R - 1) + 2 * (F - 1))

    def ring_copy(way, step, block):
        rows = pl.ds(pl.multiple_of(block * TB + way * (TB // 2), TB // 2), TB // 2)
        place = dh.at[rows, :]
        return remote(place, place, ring_s.at[way, step], ring_r.at[way, step], f, (right, left)[way])

    def ring_block(way, step):
        return lax.rem(z + NZ - step, NZ) if way == 0 else lax.rem(z + step, NZ)

    def ring(step):
        if step < NZ:
            for way in range(2):
                if step > 0:
                    ring_copy(way, step - 1, ring_block(way, step)).wait_recv()
                if step < NZ - 1:
                    ring_copy(way, step, ring_block(way, step)).start()

    def mx_copy(peer, sender):
        return remote(mx.at[:, at(peer, CB)], mch.at[at(sender, TB), :], mx_s.at[peer], mx_r.at[sender], f, peer)

    def gate_copy(n, peer_z, sender_z):
        c = (xl if n == 0 else 1 - xl) * NZ + peer_z
        return remote(
            proj.at[:, at(2 * R + c, CB)], gmn.at[n, at(sender_z, TB), :],
            gate_s.at[n, peer_z], gate_r.at[n, sender_z], f, xl * NZ + peer_z,
        )

    def w_copy(n, peer, sender):
        return remote(
            w, w2.at[pl.ds(n * CB, CB), at(sender, DB)], w_s.at[n, peer], w_r.at[n, sender], peer, (r, pr)[n]
        )

    def send_w(k):
        peer = lax.rem(f + k, F)
        w_copy(0, peer, f).start()
        w_copy(1, peer, f).start()

    ring(0)

    def send_mx(k):
        peer = lax.rem(r + k, R)
        mx_copy(peer, r).start()

    loop(1, R, send_mx)

    def send_gate(k):
        peer = lax.rem(z + k, NZ)
        gate_copy(0, peer, z).start()
        gate_copy(1, peer, z).start()

    loop(1, NZ, send_gate)
    w_copy(1, f, f).start()
    loop(1, F, send_w)

    def columns(k, part):
        tmp[:, at(k, G), :] = part.reshape(LC, G, CB)

    def pair(ref, index):
        return ref[pl.ds(index, 2)].reshape(2 * LR, CB)

    def rows_fwd(dst):
        edge = dot3(azh[...], azl[...], pair(tmp, 0)).reshape(4, LR, CB)
        dst[0:2] = edge[0:2]
        dst[LC : LC + 2] = edge[2:4]

        def step(l):
            dst[pl.ds(2 * l, 2)] = dot3(a2h[...], a2l[...], pair(tmp, 2 * l)).reshape(2, LR, CB)

        loop(1, LC // 2, step)

    def multiply(a, b, index, conjugate):
        are, aim, bre, bim = a[index], a[index + 1], b[index], b[index + 1]
        if conjugate:
            return are * bre + aim * bim, aim * bre - are * bim
        return are * bre - aim * bim, are * bim + aim * bre

    def rows_inv(a, b, conjugate):
        first, last = multiply(a, b, 0, conjugate), multiply(a, b, LC, conjugate)
        edge = jnp.concatenate(first + last, axis=0)
        tmp[0:2] = dot3(bzh[...], bzl[...], edge).reshape(2, LR, CB)

        def step(l):
            both = jnp.concatenate(multiply(a, b, 2 * l, conjugate), axis=0)
            tmp[pl.ds(2 * l, 2)] = dot3(b2h[...], b2l[...], both).reshape(2, LR, CB)

        loop(1, LC // 2, step)

    def columns_inv(k):
        return dot3(b1h[...], b1l[...], tmp[:, at(k, G), :].reshape(G * LC, CB))

    CH = G * LC
    CHUNKS = POS // CH

    def filt_step(k):
        columns(k, dot3(a1h[...], a1l[...], filt[:, at(k, CH)], dot_t))

    loop(0, CHUNKS, filt_step)
    rows_fwd(fsp)
    ring(1)

    own_mx.wait()

    def wait_mx(k):
        sender = lax.rem(r + R - k, R)
        mx_copy(r, sender).wait_recv()

    loop(1, R, wait_mx)
    ring(2)

    def plane_step(src):
        def step(k):
            x = src[at(k, CH), :]
            columns(k, dot(a1h[...], x) + dot(a1l[...], x))

        return step

    loop(0, CHUNKS, plane_step(mch))
    rows_fwd(msp)
    ring(3)
    rows_inv(msp, fsp, False)

    def conv_step(k):
        cmn[0, at(k, CH), :] = columns_inv(xl * (CHUNKS // 2) + k).astype(BF)
        cvo[at(k, CH), :] = columns_inv((1 - xl) * (CHUNKS // 2) + k).astype(BF)

    loop(0, CHUNKS // 2, conv_step)
    conv_copy = remote(cvo, cmn.at[1], x_s.at[0], x_r.at[0], f, pr)
    conv_copy.start()
    for copy in own_gate:
        copy.wait()
    own_w.wait()
    for step in range(4, NZ):
        ring(step)

    def wait_gate(k):
        sender = lax.rem(z + NZ - k, NZ)
        gate_copy(0, z, sender).wait_recv()
        gate_copy(1, z, sender).wait_recv()

    loop(1, NZ, wait_gate)

    def wait_w(k):
        sender = lax.rem(f + F - k, F)
        w_copy(0, f, sender).wait_recv()
        w_copy(1, f, sender).wait_recv()

    w_copy(1, f, f).wait_recv()
    loop(1, F, wait_w)
    conv_copy.wait_recv()

    def dgated_step(m):
        rows = at(m, CH)
        term = dot_t(dh[rows, :], w2[...])
        for n in range(2):
            d = term[:, n * CB : (n + 1) * CB]
            gate = gmn[n, rows, :].astype(F32)
            conv = cmn[n, rows, :].astype(F32)
            gt[m, pl.ds(n * CB, CB), :] = (gate * conv).T.astype(BF)
            dg[n, rows, :] = (d * conv).astype(BF)
            dconv = (d * gate).astype(BF)
            if n == 0:
                dch[pl.ds(pl.multiple_of(xl * HALF + m * CH, CH), CH), :] = dconv
            else:
                dcv[rows, :] = dconv

    loop(0, HALF // CH, dgated_step)
    dconv_copy = remote(dcv, dch.at[at(xl, HALF), :], x_s.at[1], x_r.at[1], f, pr)
    dconv_copy.start()

    def gw_copy(n, peer, slot):
        return remote(gws.at[peer, n], gwr.at[slot], gw_s.at[n, peer], gw_r.at[slot], peer, (r, pr)[n])

    def gw_step(k):
        peer = lax.rem(f + k, F)
        total = jnp.zeros((2 * CB, DB), F32)
        for m in range(HALF // CH):
            total = total + dot(gt[m], dh[pl.ds(m * CH, CH), at(peer, DB)])
        piece = total.astype(BF)
        gws[peer, 0] = piece[:CB]
        gws[peer, 1] = piece[CB:]
        gw_copy(1, peer, F + f).start()

    def gw_send_step(k):
        gw_step(k)
        gw_copy(0, lax.rem(f + k, F), f).start()

    loop(1, F, gw_send_step)
    gw_step(0)

    def dg_copy(n, peer_z, channel):
        return remote(
            dg.at[n, at(peer_z, TB), :], out.at[:, at(2 * R + channel, CB)],
            dg_s.at[n, peer_z], dg_r.at[channel], f, xl * NZ + peer_z,
        )

    own_dg = [
        pltpu.make_async_copy(dg.at[n, at(z, TB), :], out.at[:, at(2 * R + c, CB)], local.at[5 + n])
        for n, c in enumerate((r, pr))
    ]
    for copy in own_dg:
        copy.start()

    def send_dg(k):
        peer = lax.rem(z + k, NZ)
        dg_copy(0, peer, r).start()
        dg_copy(1, peer, pr).start()

    loop(1, NZ, send_dg)

    dconv_copy.wait_recv()
    loop(0, CHUNKS, plane_step(dch))
    rows_fwd(dsp)
    rows_inv(dsp, fsp, True)

    def dmixed_step(k):
        dms[at(k, CH), :] = columns_inv(k).astype(BF)

    loop(0, CHUNKS, dmixed_step)

    def dm_copy(peer, sender):
        return remote(dms.at[at(peer, TB), :], dmt.at[:, at(sender, CB)], dm_s.at[peer], dm_r.at[sender], f, peer)

    loop(1, R, lambda k: dm_copy(lax.rem(r + k, R), r).start())
    own_dm = pltpu.make_async_copy(dms.at[at(r, TB), :], dmt.at[:, at(r, CB)], local.at[7])
    own_dm.start()

    rows_inv(dsp, msp, True)

    def gf_step(k):
        gfs[at(k, CH), :] = columns_inv(k).astype(BF)

    loop(0, CHUNKS, gf_step)

    def gf_copy(peer, sender):
        return remote(gfs.at[at(peer, PB), :], gfr.at[sender], gf_s.at[peer], gf_r.at[sender], peer, r)

    loop(1, F, lambda k: gf_copy(lax.rem(f + k, F), f).start())

    def finish(c):
        cols = at(c, CB)
        d = dmt[:, cols].astype(F32)
        out[:, cols] = (d * gate_a[:, cols].astype(F32)).astype(BF)
        out[:, at(R + c, CB)] = (d * value[:, cols].astype(F32)).astype(BF)

    own_dm.wait()
    finish(r)

    def dm_step(k):
        sender = lax.rem(r + R - k, R)
        dm_copy(r, sender).wait_recv()
        finish(sender)

    loop(1, R, dm_step)

    gw_out[...] = gws[f, 0].astype(F32)

    def gw_other(sender):
        gw_copy(1, f, F + sender).wait_recv()
        gw_out[...] += gwr[F + sender].astype(F32)

    def gw_arrive(k):
        sender = lax.rem(f + F - k, F)
        gw_copy(0, f, sender).wait_recv()
        gw_out[...] += gwr[sender].astype(F32)
        gw_other(sender)

    loop(1, F, gw_arrive)
    gw_other(f)
    gw_out[...] = gw_out[...] * (1.0 / F)

    gfr[f] = gfs[at(f, PB), :]

    def gf_arrive(k):
        gf_copy(f, lax.rem(f + F - k, F)).wait_recv()

    loop(1, F, gf_arrive)
    total = gfr[0].astype(F32)
    for n in range(1, F):
        total = total + gfr[n].astype(F32)
    gf_out[...] = total.T * (1.0 / F)

    for copy in own_dg:
        copy.wait()

    def dg_arrive(k):
        sender = lax.rem(z + NZ - k, NZ)
        dg_copy(0, z, xl * NZ + sender).wait_recv()
        dg_copy(1, z, (1 - xl) * NZ + sender).wait_recv()

    loop(1, NZ, dg_arrive)

    for step in range(NZ - 1):
        for way in range(2):
            ring_copy(way, step, ring_block(way, step)).wait_send()

    def row_sent(k):
        peer = lax.rem(r + k, R)
        mx_copy(peer, r).wait_send()
        dm_copy(peer, r).wait_send()

    loop(1, R, row_sent)

    def z_sent(k):
        peer = lax.rem(z + k, NZ)
        for n in range(2):
            gate_copy(n, peer, z).wait_send()
            dg_copy(n, peer, (r, pr)[n]).wait_send()

    loop(1, NZ, z_sent)

    def plane_sent(k):
        peer = lax.rem(f + k, F)
        for n in range(2):
            w_copy(n, peer, f).wait_send()
            gw_copy(n, peer, n * F + f).wait_send()
        gf_copy(peer, f).wait_send()

    loop(1, F, plane_sent)
    w_copy(1, f, f).wait_send()
    gw_copy(1, f, F + f).wait_send()
    conv_copy.wait_send()
    dconv_copy.wait_send()


def local(R, F, proj, dout, filt, w):
    proj, dout = proj.reshape(proj.shape[1:]), dout.reshape(dout.shape[1:])
    D = dout.shape[1]
    NZ = R // 2
    TB, CB, DB, PB = POS // R, D // R, D // F, POS // F
    tables = [jnp.asarray(t) for t in build_tables()]
    vmem = pl.BlockSpec(memory_space=pltpu.VMEM)
    hbm = pl.BlockSpec(memory_space=pl.ANY)
    dma = pltpu.SemaphoreType.DMA
    spectrum = pltpu.VMEM((LC + 2, LR, CB), F32)
    grads = pl.pallas_call(
        functools.partial(kernel, R, F, D),
        out_shape=(
            jax.ShapeDtypeStruct((TB, 3 * D), BF),
            jax.ShapeDtypeStruct((CB, DB), F32),
            jax.ShapeDtypeStruct((CB, PB), F32),
        ),
        in_specs=[
            hbm, hbm, hbm, vmem,
        ] + [vmem] * len(tables),
        out_specs=(vmem, vmem, vmem),
        scratch_shapes=[
            pltpu.VMEM((TB, D), BF), pltpu.VMEM((TB, D), BF),
            pltpu.VMEM((TB, D), BF),
            pltpu.VMEM((POS, CB), BF),
            pltpu.VMEM((2, HALF, CB), BF),
            pltpu.VMEM((2, HALF, CB), BF),
            pltpu.VMEM((HALF, CB), BF),
            pltpu.VMEM((HALF, D), BF),
            pltpu.VMEM((2 * CB, D), BF),
            spectrum, spectrum, spectrum,
            pltpu.VMEM((LC, LR, CB), F32),
            pltpu.VMEM((HALF // (G * LC), 2 * CB, G * LC), BF),
            pltpu.VMEM((HALF, CB), BF),
            pltpu.VMEM((POS, CB), BF),
            pltpu.VMEM((2, HALF, CB), BF),
            pltpu.VMEM((POS, CB), BF),
            pltpu.VMEM((TB, D), BF),
            pltpu.VMEM((F, 2, CB, DB), BF),
            pltpu.VMEM((2 * F, CB, DB), BF),
            pltpu.VMEM((POS, CB), BF),
            pltpu.VMEM((F, PB, CB), BF),
            dma((10,)),
            dma((2, NZ)), dma((2, NZ)),
            dma((R,)), dma((R,)),
            dma((2, NZ)), dma((2, NZ)),
            dma((2, F)), dma((2, F)),
            dma((2,)), dma((2,)),
            dma((2, NZ)), dma((R,)),
            dma((R,)), dma((R,)),
            dma((2, F)), dma((2 * F,)),
            dma((F,)), dma((F,)),
        ],
        compiler_params=pltpu.CompilerParams(
            collective_id=0, has_side_effects=True, vmem_limit_bytes=62 * 1024 * 1024
        ),
    )(proj, dout, w, filt, *tables)
    return grads[0][None], grads[1], grads[2]


def solution(mesh):
    placed = (P("frame", "row", None), P("frame", "row", None), P("row", None), P("row", "frame"))
    return jax.shard_map(
        functools.partial(local, mesh.shape["row"], mesh.shape["frame"]),
        mesh=mesh,
        in_specs=placed,
        out_specs=(P("frame", "row", None), P("row", "frame"), P("row", "frame")),
        check_vma=False,
    )
```

```python
import functools

import jax
import jax.numpy as jnp
import ml_dtypes
import numpy as np
from jax import lax
from jax.experimental import pallas as pl
from jax.experimental.pallas import tpu as pltpu
from jax.sharding import PartitionSpec as P

LR = 64
LC = 32
POS = LR * LC
HALF = POS // 2
RIGHT = 8
SUB = 2
G = 8
MESH = pl.DeviceIdType.MESH
BF = jnp.bfloat16
F32 = jnp.float32


def split_table(table):
    high = table.astype(ml_dtypes.bfloat16)
    low = (table - high.astype(np.float64)).astype(ml_dtypes.bfloat16)
    return high, low


def build_tables():
    j = np.arange(LC)
    fwd = np.zeros((LC, LC))
    inv = np.zeros((LC, LC))
    fwd[0], inv[:, 0] = 1.0, 1.0
    fwd[1] = np.cos(np.pi * j)
    inv[:, 1] = np.cos(np.pi * j)
    for l in range(1, LC // 2):
        angle = 2 * np.pi * ((j * l) % LC) / LC
        fwd[2 * l], fwd[2 * l + 1] = np.cos(angle), -np.sin(angle)
        inv[:, 2 * l], inv[:, 2 * l + 1] = 2 * np.cos(angle), -2 * np.sin(angle)
    inv = inv / POS
    eye = np.eye(G)
    col_fwd = np.einsum("qj,ab->qabj", fwd, eye).reshape(G * LC, G * LC)
    col_inv = np.einsum("jq,ab->ajqb", inv, eye).reshape(G * LC, G * LC)
    i = np.arange(LR)
    angle = 2 * np.pi * ((i[:, None] * i[None, :]) % LR) / LR
    c, s = np.cos(angle), np.sin(angle)
    o = np.zeros_like(c)
    row_fwd = np.block([[c, s], [-s, c]])
    row_inv = np.block([[c, -s], [s, c]])
    edge_fwd = np.block([[c, o], [-s, o], [o, c], [o, -s]])
    edge_inv = np.block([[c, -s, o, o], [o, o, c, -s]])
    out = []
    for table in (col_fwd, row_fwd, edge_fwd, row_inv, edge_inv, col_inv):
        out.extend(split_table(table))
    return tuple(out)


def split(x):
    high = x.astype(BF)
    return high, (x - high.astype(F32)).astype(BF)


def dot(a, b):
    return jnp.dot(a, b, preferred_element_type=F32)


def dot_t(a, b):
    return lax.dot_general(a, b, (((1,), (1,)), ((), ())), preferred_element_type=F32)


def dot3(high, low, x, product=dot):
    x_high, x_low = split(x)
    return product(high, x_high) + product(high, x_low) + product(low, x_high)


def kernel(
    R, F, D, CR,
    proj, dout, w, filt,
    a1h, a1l, a2h, a2l, azh, azl, b2h, b2l, bzh, bzl, b1h, b1l,
    out, gw_out, gf_out,
    value, gate_a, mx, mch, gmn, cmn, cvo, dh, w2, fsp, msp, dsp, tmp, acc, gt, dcv, dch, dg, dms, dmt,
    gwx, gwy, gws, gwr, gff, gfx, gfy, gfs, gfr,
    local, ring_s, ring_r, mx_s, mx_r, gate_s, gate_r, w_s, w_r, x_s, x_r, dg_s, dg_r, dm_s, dm_r,
    gwx_s, gwx_r, gw_s, gw_r, gfx_s, gfx_r, gf_s, gf_r,
):
    NZ = R // 2
    TB, CB, DB, PB = POS // R, D // R, D // F, POS // F
    f, r = lax.axis_index("frame"), lax.axis_index("row")
    xl, z = lax.div(r, NZ), lax.rem(r, NZ)
    pr = (1 - xl) * NZ + z
    right = xl * NZ + lax.rem(z + 1, NZ)
    left = xl * NZ + lax.rem(z + NZ - 1, NZ)
    FC = F // 2
    chip, core = lax.div(f, 2), lax.rem(f, 2)
    twin = f + 1 - 2 * core

    def at(index, size):
        return pl.ds(pl.multiple_of(index * size, size), size)

    def remote(src, dst, send, recv, frame, row):
        return pltpu.make_async_remote_copy(
            src_ref=src, dst_ref=dst, send_sem=send, recv_sem=recv,
            device_id={"frame": frame, "row": row}, device_id_type=MESH,
        )

    def loop(start, stop, step):
        def body(k, carry):
            step(k)
            return carry

        lax.fori_loop(start, stop, body, 0)

    own_dout = pltpu.make_async_copy(dout, dh.at[at(z, TB), :], local.at[0])
    own_w = pltpu.make_async_copy(w, w2.at[pl.ds(0, CB), at(f, DB)], local.at[1])
    own_gate = [
        pltpu.make_async_copy(proj.at[:, at(2 * R + c, CB)], gmn.at[n, at(z, TB), :], local.at[2 + n])
        for n, c in enumerate((r, pr))
    ]
    own_value = pltpu.make_async_copy(proj.at[:, pl.ds(0, D)], value, local.at[8])
    own_a = pltpu.make_async_copy(proj.at[:, pl.ds(D, D)], gate_a, local.at[9])
    own_value.start()
    own_a.start()
    own_dout.start()
    own_w.start()
    for copy in own_gate:
        copy.start()

    barrier = pltpu.get_barrier_semaphore()

    def greet(frame, row):
        pl.semaphore_signal(barrier, inc=1, device_id={"frame": frame, "row": row}, device_id_type=MESH)

    loop(1, R, lambda k: greet(f, lax.rem(r + k, R)))

    def greet_plane(k):
        greet(lax.rem(f + k, F), r)
        greet(lax.rem(f + k, F), pr)

    loop(1, F, greet_plane)

    own_value.wait()
    own_a.wait()
    mx[...] = (value[...].astype(F32) * gate_a[...].astype(F32)).astype(BF)
    own_mx = pltpu.make_async_copy(mx.at[:, at(r, CB)], mch.at[at(r, TB), :], local.at[4])
    own_mx.start()
    own_dout.wait()
    pl.semaphore_wait(barrier, (R - 1) + 2 * (F - 1))

    def ring_part(way, sub):
        width = (CR if way == 0 else D - CR) // SUB
        return pl.ds((0 if way == 0 else CR) + sub * width, width)

    def ring_copy(way, sub, step, block):
        place = dh.at[at(block, TB), ring_part(way, sub)]
        n = way * SUB + sub
        return remote(place, place, ring_s.at[n, step], ring_r.at[n, step], f, (right, left)[way])

    def ring_block(way, step):
        return lax.rem(z + NZ - step, NZ) if way == 0 else lax.rem(z + step, NZ)

    def ring(step):
        if step < NZ:
            for sub in range(SUB):
                for way in range(2):
                    if step > 0:
                        ring_copy(way, sub, step - 1, ring_block(way, step)).wait_recv()
                    if step < NZ - 1:
                        ring_copy(way, sub, step, ring_block(way, step)).start()

    def mx_copy(peer, sender):
        return remote(mx.at[:, at(peer, CB)], mch.at[at(sender, TB), :], mx_s.at[peer], mx_r.at[sender], f, peer)

    def gate_copy(n, peer_z, sender_z):
        c = (xl if n == 0 else 1 - xl) * NZ + peer_z
        return remote(
            proj.at[:, at(2 * R + c, CB)], gmn.at[n, at(sender_z, TB), :],
            gate_s.at[n, peer_z], gate_r.at[n, sender_z], f, xl * NZ + peer_z,
        )

    def w_copy(n, peer, sender):
        return remote(
            w, w2.at[pl.ds(n * CB, CB), at(sender, DB)], w_s.at[n, peer], w_r.at[n, sender], peer, (r, pr)[n]
        )

    def send_w(k):
        peer = lax.rem(f + k, F)
        w_copy(0, peer, f).start()
        w_copy(1, peer, f).start()

    ring(0)

    def send_mx(k):
        peer = lax.rem(r + k, R)
        mx_copy(peer, r).start()

    loop(1, R, send_mx)

    def send_gate(k):
        peer = lax.rem(z + k, NZ)
        gate_copy(0, peer, z).start()
        gate_copy(1, peer, z).start()

    loop(1, NZ, send_gate)
    w_copy(1, f, f).start()
    loop(1, F, send_w)

    def columns(k, part):
        tmp[:, at(k, G), :] = part.reshape(LC, G, CB)

    def pair(ref, index):
        return ref[pl.ds(index, 2)].reshape(2 * LR, CB)

    def rows_fwd(dst):
        edge = dot3(azh[...], azl[...], pair(tmp, 0)).reshape(4, LR, CB)
        dst[0:2] = edge[0:2]
        dst[LC : LC + 2] = edge[2:4]

        def step(l):
            dst[pl.ds(2 * l, 2)] = dot3(a2h[...], a2l[...], pair(tmp, 2 * l)).reshape(2, LR, CB)

        loop(1, LC // 2, step)

    def multiply(a, b, index, conjugate):
        are, aim, bre, bim = a[index], a[index + 1], b[index], b[index + 1]
        if conjugate:
            return are * bre + aim * bim, aim * bre - are * bim
        return are * bre - aim * bim, are * bim + aim * bre

    def rows_inv(a, b, conjugate):
        first, last = multiply(a, b, 0, conjugate), multiply(a, b, LC, conjugate)
        edge = jnp.concatenate(first + last, axis=0)
        tmp[0:2] = dot3(bzh[...], bzl[...], edge).reshape(2, LR, CB)

        def step(l):
            both = jnp.concatenate(multiply(a, b, 2 * l, conjugate), axis=0)
            tmp[pl.ds(2 * l, 2)] = dot3(b2h[...], b2l[...], both).reshape(2, LR, CB)

        loop(1, LC // 2, step)

    def columns_inv(k):
        return dot3(b1h[...], b1l[...], tmp[:, at(k, G), :].reshape(G * LC, CB))

    CH = G * LC
    CHUNKS = POS // CH

    def filt_step(k):
        columns(k, dot3(a1h[...], a1l[...], filt[:, at(k, CH)], dot_t))

    loop(0, CHUNKS, filt_step)
    ring(1)
    rows_fwd(fsp)

    own_mx.wait()

    def wait_mx(k):
        sender = lax.rem(r + R - k, R)
        mx_copy(r, sender).wait_recv()

    loop(1, R, wait_mx)
    ring(2)

    def plane_step(src):
        def step(k):
            x = src[at(k, CH), :]
            columns(k, dot(a1h[...], x) + dot(a1l[...], x))

        return step

    loop(0, CHUNKS, plane_step(mch))
    rows_fwd(msp)
    ring(3)
    rows_inv(msp, fsp, False)

    def conv_step(k):
        cmn[0, at(k, CH), :] = columns_inv(xl * (CHUNKS // 2) + k).astype(BF)
        cvo[at(k, CH), :] = columns_inv((1 - xl) * (CHUNKS // 2) + k).astype(BF)

    loop(0, CHUNKS // 2, conv_step)
    conv_copy = remote(cvo, cmn.at[1], x_s.at[NZ], x_r.at[NZ], f, pr)
    conv_copy.start()
    for copy in own_gate:
        copy.wait()
    own_w.wait()
    ring(4)

    def wait_w(k):
        sender = lax.rem(f + F - k, F)
        w_copy(0, f, sender).wait_recv()
        w_copy(1, f, sender).wait_recv()

    w_copy(1, f, f).wait_recv()
    loop(1, F, wait_w)

    def part(t):
        if t == 0:
            acc[at(z, TB), :] = dot_t(dh[at(z, TB), :], w2[...])
            return
        for way in range(2):
            rows = at(ring_block(way, t), TB)
            cols = pl.ds(0, CR) if way == 0 else pl.ds(CR, D - CR)
            term = dot_t(dh[rows, cols], w2[:, cols])
            if t < NZ // 2 or (t == NZ // 2 and way == 0):
                acc[rows, :] = term
            else:
                acc[rows, :] += term

    def dconv_copy(block, half):
        rows = pl.ds(pl.multiple_of(half * HALF + block * TB, TB), TB)
        return remote(dcv.at[at(block, TB), :], dch.at[rows, :], x_s.at[block], x_r.at[block], f, pr)

    def dg_copy(n, peer_z, channel):
        return remote(
            dg.at[n, at(peer_z, TB), :], out.at[:, at(2 * R + channel, CB)],
            dg_s.at[n, peer_z], dg_r.at[channel], f, xl * NZ + peer_z,
        )

    own_dg = [
        pltpu.make_async_copy(dg.at[n, at(z, TB), :], out.at[:, at(2 * R + c, CB)], local.at[5 + n])
        for n, c in enumerate((r, pr))
    ]

    def finalize(block, own):
        rows = at(block, TB)
        for n in range(2):
            d = acc[rows, n * CB : (n + 1) * CB]
            gate = gmn[n, rows, :].astype(F32)
            conv = cmn[n, rows, :].astype(F32)
            gt[n * CB : (n + 1) * CB, rows] = (gate * conv).T.astype(BF)
            dg[n, rows, :] = (d * conv).astype(BF)
            dconv = (d * gate).astype(BF)
            if n == 0:
                dch[pl.ds(pl.multiple_of(xl * HALF + block * TB, TB), TB), :] = dconv
            else:
                dcv[rows, :] = dconv
        dconv_copy(block, xl).start()
        if own:
            for copy in own_dg:
                copy.start()
        else:
            dg_copy(0, block, r).start()
            dg_copy(1, block, pr).start()

    def wait_gate(k):
        sender = lax.rem(z + NZ - k, NZ)
        gate_copy(0, z, sender).wait_recv()
        gate_copy(1, z, sender).wait_recv()

    def step_done(t):
        part(t)
        if t == 0:
            finalize(z, True)
        elif t == NZ // 2:
            finalize(ring_block(0, t), False)
        elif t > NZ // 2:
            finalize(ring_block(0, t), False)
            finalize(ring_block(1, t), False)

    for t in range(1, min(4, NZ)):
        part(t)
    loop(1, NZ, wait_gate)
    conv_copy.wait_recv()
    step_done(0)
    if NZ <= 4:
        for t in range(NZ // 2, NZ):
            finalize(ring_block(0, t), False)
            if t > NZ // 2:
                finalize(ring_block(1, t), False)
    ring(5)
    for t in range(4, NZ):
        step_done(t)
        ring(t + 2)

    def gw_partial(cols):
        return dot(gt[...], dh[:, at(cols, DB)])

    def gwx_copy(j):
        return remote(gwx.at[j], gwy.at[j], gwx_s.at[j], gwx_r.at[j], twin, r)

    def gwx_step(k):
        j = lax.rem(chip + k, FC)
        gwx[j] = gw_partial(2 * j + 1 - core).astype(BF)
        gwx_copy(j).start()

    loop(0, FC, gwx_step)

    def gw_copy(n, peer, sender):
        return remote(gws.at[peer, n], gwr.at[n, sender], gw_s.at[n, peer], gw_r.at[n, sender], 2 * peer + core, (r, pr)[n])

    def gw_step(j):
        total = gw_partial(2 * j + core)
        gwx_copy(j).wait_recv()
        piece = (total + gwy[j].astype(F32)).astype(BF)
        gws[j, 0] = piece[:CB]
        gws[j, 1] = piece[CB:]
        gw_copy(1, j, chip).start()

    def gw_send_step(k):
        j = lax.rem(chip + k, FC)
        gw_step(j)
        gw_copy(0, j, chip).start()

    loop(1, FC, gw_send_step)
    gw_step(chip)

    loop(0, NZ, lambda k: dconv_copy(k, 1 - xl).wait_recv())
    loop(0, CHUNKS, plane_step(dch))
    rows_fwd(dsp)
    rows_inv(dsp, fsp, True)

    def dmixed_step(k):
        dms[at(k, CH), :] = columns_inv(k).astype(BF)

    loop(0, CHUNKS, dmixed_step)

    def dm_copy(peer, sender):
        return remote(dms.at[at(peer, TB), :], dmt.at[:, at(sender, CB)], dm_s.at[peer], dm_r.at[sender], f, peer)

    loop(1, R, lambda k: dm_copy(lax.rem(r + k, R), r).start())
    own_dm = pltpu.make_async_copy(dms.at[at(r, TB), :], dmt.at[:, at(r, CB)], local.at[7])
    own_dm.start()

    rows_inv(dsp, msp, True)

    def gf_step(k):
        gff[at(k, CH), :] = columns_inv(k)

    loop(0, CHUNKS, gf_step)

    def gfx_copy(j):
        return remote(gfx.at[j], gfy.at[j], gfx_s.at[j], gfx_r.at[j], twin, r)

    def gfx_step(j):
        gfx[j] = gff[at(2 * j + 1 - core, PB), :].astype(BF)
        gfx_copy(j).start()

    loop(0, FC, gfx_step)

    def gf_copy(peer, sender):
        return remote(gfs.at[peer], gfr.at[sender], gf_s.at[peer], gf_r.at[sender], 2 * peer + core, r)

    def gf_sum(j):
        gfx_copy(j).wait_recv()
        gfs[j] = (gff[at(2 * j + core, PB), :] + gfy[j].astype(F32)).astype(BF)

    def gf_send_step(k):
        j = lax.rem(chip + k, FC)
        gf_sum(j)
        gf_copy(j, chip).start()

    loop(1, FC, gf_send_step)
    gf_sum(chip)

    def finish(c):
        cols = at(c, CB)
        d = dmt[:, cols].astype(F32)
        out[:, cols] = (d * gate_a[:, cols].astype(F32)).astype(BF)
        out[:, at(R + c, CB)] = (d * value[:, cols].astype(F32)).astype(BF)

    own_dm.wait()
    finish(r)

    def dm_step(k):
        sender = lax.rem(r + R - k, R)
        dm_copy(r, sender).wait_recv()
        finish(sender)

    loop(1, R, dm_step)

    gw_out[...] = gws[chip, 0].astype(F32)

    def gw_add(n, sender):
        gw_copy(n, chip, sender).wait_recv()
        gw_out[...] += gwr[n, sender].astype(F32)

    def gw_arrive(k):
        sender = lax.rem(chip + FC - k, FC)
        gw_add(0, sender)
        gw_add(1, sender)

    loop(1, FC, gw_arrive)
    gw_add(1, chip)
    gw_out[...] = gw_out[...] * (1.0 / F)

    gfr[chip] = gfs[chip]
    loop(1, FC, lambda k: gf_copy(chip, lax.rem(chip + FC - k, FC)).wait_recv())
    total = gfr[0].astype(F32)
    for n in range(1, FC):
        total = total + gfr[n].astype(F32)
    gf_out[...] = total.T * (1.0 / F)

    for copy in own_dg:
        copy.wait()

    def dg_arrive(k):
        sender = lax.rem(z + NZ - k, NZ)
        dg_copy(0, z, xl * NZ + sender).wait_recv()
        dg_copy(1, z, (1 - xl) * NZ + sender).wait_recv()

    loop(1, NZ, dg_arrive)

    for step in range(NZ - 1):
        for way in range(2):
            for sub in range(SUB):
                ring_copy(way, sub, step, ring_block(way, step)).wait_send()

    def row_sent(k):
        peer = lax.rem(r + k, R)
        mx_copy(peer, r).wait_send()
        dm_copy(peer, r).wait_send()

    loop(1, R, row_sent)

    def z_sent(k):
        peer = lax.rem(z + k, NZ)
        for n in range(2):
            gate_copy(n, peer, z).wait_send()
            dg_copy(n, peer, (r, pr)[n]).wait_send()

    loop(1, NZ, z_sent)
    loop(0, NZ, lambda k: dconv_copy(k, xl).wait_send())

    def plane_sent(k):
        peer = lax.rem(f + k, F)
        for n in range(2):
            w_copy(n, peer, f).wait_send()

    loop(1, F, plane_sent)

    def chip_sent(k):
        peer = lax.rem(chip + k, FC)
        gw_copy(0, peer, chip).wait_send()
        gf_copy(peer, chip).wait_send()

    loop(1, FC, chip_sent)

    def twin_sent(j):
        gw_copy(1, j, chip).wait_send()
        gwx_copy(j).wait_send()
        gfx_copy(j).wait_send()

    loop(0, FC, twin_sent)
    w_copy(1, f, f).wait_send()
    conv_copy.wait_send()


def local(R, F, proj, dout, filt, w):
    proj, dout = proj.reshape(proj.shape[1:]), dout.reshape(dout.shape[1:])
    D = dout.shape[1]
    NZ = R // 2
    TB, CB, DB, PB = POS // R, D // R, D // F, POS // F
    CR = D * RIGHT // 16 // (128 * SUB) * (128 * SUB)
    tables = [jnp.asarray(t) for t in build_tables()]
    vmem = pl.BlockSpec(memory_space=pltpu.VMEM)
    hbm = pl.BlockSpec(memory_space=pl.ANY)
    dma = pltpu.SemaphoreType.DMA
    spectrum = pltpu.VMEM((LC + 2, LR, CB), F32)
    grads = pl.pallas_call(
        functools.partial(kernel, R, F, D, CR),
        out_shape=(
            jax.ShapeDtypeStruct((TB, 3 * D), BF),
            jax.ShapeDtypeStruct((CB, DB), F32),
            jax.ShapeDtypeStruct((CB, PB), F32),
        ),
        in_specs=[
            hbm, hbm, hbm, vmem,
        ] + [vmem] * len(tables),
        out_specs=(vmem, vmem, vmem),
        scratch_shapes=[
            pltpu.VMEM((TB, D), BF), pltpu.VMEM((TB, D), BF),
            pltpu.VMEM((TB, D), BF),
            pltpu.VMEM((POS, CB), BF),
            pltpu.VMEM((2, HALF, CB), BF),
            pltpu.VMEM((2, HALF, CB), BF),
            pltpu.VMEM((HALF, CB), BF),
            pltpu.VMEM((HALF, D), BF),
            pltpu.VMEM((2 * CB, D), BF),
            spectrum, spectrum, spectrum,
            pltpu.VMEM((LC, LR, CB), F32),
            pltpu.VMEM((HALF, 2 * CB), F32),
            pltpu.VMEM((2 * CB, HALF), BF),
            pltpu.VMEM((HALF, CB), BF),
            pltpu.VMEM((POS, CB), BF),
            pltpu.VMEM((2, HALF, CB), BF),
            pltpu.VMEM((POS, CB), BF),
            pltpu.VMEM((TB, D), BF),
            pltpu.VMEM((F // 2, 2 * CB, DB), BF), pltpu.VMEM((F // 2, 2 * CB, DB), BF),
            pltpu.VMEM((F // 2, 2, CB, DB), BF), pltpu.VMEM((2, F // 2, CB, DB), BF),
            pltpu.VMEM((POS, CB), F32),
            pltpu.VMEM((F // 2, PB, CB), BF), pltpu.VMEM((F // 2, PB, CB), BF),
            pltpu.VMEM((F // 2, PB, CB), BF), pltpu.VMEM((F // 2, PB, CB), BF),
            dma((10,)),
            dma((2 * SUB, NZ)), dma((2 * SUB, NZ)),
            dma((R,)), dma((R,)),
            dma((2, NZ)), dma((2, NZ)),
            dma((2, F)), dma((2, F)),
            dma((NZ + 1,)), dma((NZ + 1,)),
            dma((2, NZ)), dma((R,)),
            dma((R,)), dma((R,)),
            dma((F // 2,)), dma((F // 2,)), dma((2, F // 2)), dma((2, F // 2)),
            dma((F // 2,)), dma((F // 2,)), dma((F // 2,)), dma((F // 2,)),
        ],
        compiler_params=pltpu.CompilerParams(
            collective_id=0, has_side_effects=True, vmem_limit_bytes=62 * 1024 * 1024
        ),
    )(proj, dout, w, filt, *tables)
    return grads[0][None], grads[1], grads[2]


def solution(mesh):
    placed = (P("frame", "row", None), P("frame", "row", None), P("row", None), P("row", "frame"))
    return jax.shard_map(
        functools.partial(local, mesh.shape["row"], mesh.shape["frame"]),
        mesh=mesh,
        in_specs=placed,
        out_specs=(P("frame", "row", None), P("row", "frame"), P("row", "frame")),
        check_vma=False,
    )
```

```python
import functools

import jax
import jax.numpy as jnp
import ml_dtypes
import numpy as np
from jax import lax
from jax.experimental import pallas as pl
from jax.experimental.pallas import tpu as pltpu
from jax.sharding import PartitionSpec as P

LR = 64
LC = 32
POS = LR * LC
HALF = POS // 2
RIGHT = 8
SUB = 2
G = 8
MESH = pl.DeviceIdType.MESH
BF = jnp.bfloat16
F32 = jnp.float32


def split_table(table):
    high = table.astype(ml_dtypes.bfloat16)
    low = (table - high.astype(np.float64)).astype(ml_dtypes.bfloat16)
    return high, low


def build_tables():
    j = np.arange(LC)
    fwd = np.zeros((LC, LC))
    inv = np.zeros((LC, LC))
    fwd[0], inv[:, 0] = 1.0, 1.0
    fwd[1] = np.cos(np.pi * j)
    inv[:, 1] = np.cos(np.pi * j)
    for l in range(1, LC // 2):
        angle = 2 * np.pi * ((j * l) % LC) / LC
        fwd[2 * l], fwd[2 * l + 1] = np.cos(angle), -np.sin(angle)
        inv[:, 2 * l], inv[:, 2 * l + 1] = 2 * np.cos(angle), -2 * np.sin(angle)
    inv = inv / POS
    eye = np.eye(G)
    col_fwd = np.einsum("qj,ab->qabj", fwd, eye).reshape(G * LC, G * LC)
    col_inv = np.einsum("jq,ab->ajqb", inv, eye).reshape(G * LC, G * LC)
    i = np.arange(LR)
    angle = 2 * np.pi * ((i[:, None] * i[None, :]) % LR) / LR
    c, s = np.cos(angle), np.sin(angle)
    o = np.zeros_like(c)
    row_fwd = np.block([[c, s], [-s, c]])
    row_inv = np.block([[c, -s], [s, c]])
    edge_fwd = np.block([[c, o], [-s, o], [o, c], [o, -s]])
    edge_inv = np.block([[c, -s, o, o], [o, o, c, -s]])
    out = []
    for table in (col_fwd, row_fwd, edge_fwd, row_inv, edge_inv, col_inv):
        out.extend(split_table(table))
    return tuple(out)


def split(x):
    high = x.astype(BF)
    return high, (x - high.astype(F32)).astype(BF)


def dot(a, b):
    return jnp.dot(a, b, preferred_element_type=F32)


def dot_t(a, b):
    return lax.dot_general(a, b, (((1,), (1,)), ((), ())), preferred_element_type=F32)


def dot3(high, low, x, product=dot):
    x_high, x_low = split(x)
    return product(high, x_high) + product(high, x_low) + product(low, x_high)


def kernel(
    R, F, D, CR,
    proj, dout, w, filt_hbm, t0, t1, t2, t3, t4, t5, t6, t7, t8, t9, t10, t11,
    dmt, dgt, gw_out, gf_out,
    filt, a1h, a1l, a2h, a2l, azh, azl, b2h, b2l, bzh, bzl, b1h, b1l,
    value, gate_a, mx, mch, gmn, cmn, cvo, dh, w2, fsp, msp, dsp, tmp, acc, gt, dcv, dch, dg, dms,
    gwx, gwy, gws, gwr, gff, gfx, gfy, gfs, gfr,
    local, ring_s, ring_r, mx_s, mx_r, gate_s, gate_r, w_s, w_r, x_s, x_r, dg_s, dg_r, dm_s, dm_r,
    gwx_s, gwx_r, gw_s, gw_r, gfx_s, gfx_r, gf_s, gf_r,
):
    NZ = R // 2
    TB, CB, DB, PB = POS // R, D // R, D // F, POS // F
    f, r = lax.axis_index("frame"), lax.axis_index("row")
    xl, z = lax.div(r, NZ), lax.rem(r, NZ)
    pr = (1 - xl) * NZ + z
    right = xl * NZ + lax.rem(z + 1, NZ)
    left = xl * NZ + lax.rem(z + NZ - 1, NZ)
    FC = F // 2
    chip, core = lax.div(f, 2), lax.rem(f, 2)
    twin = f + 1 - 2 * core

    def at(index, size):
        return pl.ds(pl.multiple_of(index * size, size), size)

    def remote(src, dst, send, recv, frame, row):
        return pltpu.make_async_remote_copy(
            src_ref=src, dst_ref=dst, send_sem=send, recv_sem=recv,
            device_id={"frame": frame, "row": row}, device_id_type=MESH,
        )

    def loop(start, stop, step):
        def body(k, carry):
            step(k)
            return carry

        lax.fori_loop(start, stop, body, 0)

    barrier = pltpu.get_barrier_semaphore()

    def greet(frame, row):
        pl.semaphore_signal(barrier, inc=1, device_id={"frame": frame, "row": row}, device_id_type=MESH)

    loop(1, R, lambda k: greet(f, lax.rem(r + k, R)))

    def greet_plane(k):
        greet(lax.rem(f + k, F), r)
        greet(lax.rem(f + k, F), pr)

    loop(1, F, greet_plane)

    own_dout = pltpu.make_async_copy(dout, dh.at[at(z, TB), :], local.at[0])
    own_w = pltpu.make_async_copy(w, w2.at[pl.ds(0, CB), at(f, DB)], local.at[1])
    own_gate = [
        pltpu.make_async_copy(proj.at[:, at(2 * R + c, CB)], gmn.at[n, at(z, TB), :], local.at[2 + n])
        for n, c in enumerate((r, pr))
    ]
    own_value = pltpu.make_async_copy(proj.at[:, pl.ds(0, D)], value, local.at[8])
    own_a = pltpu.make_async_copy(proj.at[:, pl.ds(D, D)], gate_a, local.at[9])
    own_value.start()
    own_a.start()
    own_dout.start()
    own_w.start()
    for copy in own_gate:
        copy.start()
    own_tables = [
        pltpu.make_async_copy(pair[0], pair[1], local.at[10 + n])
        for n, pair in enumerate(
            zip(
                (filt_hbm, t0, t1, t2, t3, t4, t5, t6, t7, t8, t9, t10, t11),
                (filt, a1h, a1l, a2h, a2l, azh, azl, b2h, b2l, bzh, bzl, b1h, b1l),
            )
        )
    ]
    for copy in own_tables:
        copy.start()

    own_value.wait()
    own_a.wait()
    mx[...] = (value[...].astype(F32) * gate_a[...].astype(F32)).astype(BF)
    own_mx = pltpu.make_async_copy(mx.at[:, at(r, CB)], mch.at[at(r, TB), :], local.at[4])
    own_mx.start()
    pl.semaphore_wait(barrier, (R - 1) + 2 * (F - 1))

    def ring_part(way, sub):
        width = (CR if way == 0 else D - CR) // SUB
        return pl.ds((0 if way == 0 else CR) + sub * width, width)

    def ring_copy(way, sub, step, block):
        place = dh.at[at(block, TB), ring_part(way, sub)]
        n = way * SUB + sub
        first = dout.at[:, ring_part(way, sub)] if step == 0 else place
        return remote(first, place, ring_s.at[n, step], ring_r.at[n, step], f, (right, left)[way])

    def ring_block(way, step):
        return lax.rem(z + NZ - step, NZ) if way == 0 else lax.rem(z + step, NZ)

    def ring(step):
        if step < NZ:
            for sub in range(SUB):
                for way in range(2):
                    if step > 0:
                        ring_copy(way, sub, step - 1, ring_block(way, step)).wait_recv()
                    if step < NZ - 1:
                        ring_copy(way, sub, step, ring_block(way, step)).start()

    def mx_copy(peer, sender):
        return remote(mx.at[:, at(peer, CB)], mch.at[at(sender, TB), :], mx_s.at[peer], mx_r.at[sender], f, peer)

    def gate_copy(n, peer_z, sender_z):
        c = (xl if n == 0 else 1 - xl) * NZ + peer_z
        return remote(
            proj.at[:, at(2 * R + c, CB)], gmn.at[n, at(sender_z, TB), :],
            gate_s.at[n, peer_z], gate_r.at[n, sender_z], f, xl * NZ + peer_z,
        )

    def w_copy(n, peer, sender):
        return remote(
            w, w2.at[pl.ds(n * CB, CB), at(sender, DB)], w_s.at[n, peer], w_r.at[n, sender], peer, (r, pr)[n]
        )

    def send_w(k):
        peer = lax.rem(f + k, F)
        w_copy(0, peer, f).start()
        w_copy(1, peer, f).start()

    ring(0)

    def send_mx(k):
        peer = lax.rem(r + k, R)
        mx_copy(peer, r).start()

    loop(1, R, send_mx)

    def send_gate(k):
        peer = lax.rem(z + k, NZ)
        gate_copy(0, peer, z).start()
        gate_copy(1, peer, z).start()

    loop(1, NZ, send_gate)
    w_copy(1, f, f).start()
    loop(1, F, send_w)

    def columns(k, part):
        tmp[:, at(k, G), :] = part.reshape(LC, G, CB)

    def pair(ref, index):
        return ref[pl.ds(index, 2)].reshape(2 * LR, CB)

    def rows_fwd(dst):
        edge = dot3(azh[...], azl[...], pair(tmp, 0)).reshape(4, LR, CB)
        dst[0:2] = edge[0:2]
        dst[LC : LC + 2] = edge[2:4]

        def step(l):
            dst[pl.ds(2 * l, 2)] = dot3(a2h[...], a2l[...], pair(tmp, 2 * l)).reshape(2, LR, CB)

        loop(1, LC // 2, step)

    def multiply(a, b, index, conjugate):
        are, aim, bre, bim = a[index], a[index + 1], b[index], b[index + 1]
        if conjugate:
            return are * bre + aim * bim, aim * bre - are * bim
        return are * bre - aim * bim, are * bim + aim * bre

    def rows_inv(a, b, conjugate):
        first, last = multiply(a, b, 0, conjugate), multiply(a, b, LC, conjugate)
        edge = jnp.concatenate(first + last, axis=0)
        tmp[0:2] = dot3(bzh[...], bzl[...], edge).reshape(2, LR, CB)

        def step(l):
            both = jnp.concatenate(multiply(a, b, 2 * l, conjugate), axis=0)
            tmp[pl.ds(2 * l, 2)] = dot3(b2h[...], b2l[...], both).reshape(2, LR, CB)

        loop(1, LC // 2, step)

    def columns_inv(k):
        return dot3(b1h[...], b1l[...], tmp[:, at(k, G), :].reshape(G * LC, CB))

    CH = G * LC
    CHUNKS = POS // CH

    def filt_step(k):
        columns(k, dot3(a1h[...], a1l[...], filt[:, at(k, CH)], dot_t))

    for copy in own_tables:
        copy.wait()
    loop(0, CHUNKS, filt_step)
    ring(1)
    rows_fwd(fsp)

    own_mx.wait()

    def wait_mx(k):
        sender = lax.rem(r + R - k, R)
        mx_copy(r, sender).wait_recv()

    loop(1, R, wait_mx)
    ring(2)

    def plane_step(src):
        def step(k):
            x = src[at(k, CH), :]
            columns(k, dot(a1h[...], x) + dot(a1l[...], x))

        return step

    loop(0, CHUNKS, plane_step(mch))
    rows_fwd(msp)
    ring(3)
    rows_inv(msp, fsp, False)

    def conv_step(k):
        cmn[0, at(k, CH), :] = columns_inv(xl * (CHUNKS // 2) + k).astype(BF)
        cvo[at(k, CH), :] = columns_inv((1 - xl) * (CHUNKS // 2) + k).astype(BF)

    loop(0, CHUNKS // 2, conv_step)
    conv_copy = remote(cvo, cmn.at[1], x_s.at[NZ], x_r.at[NZ], f, pr)
    conv_copy.start()
    for copy in own_gate:
        copy.wait()
    own_w.wait()
    own_dout.wait()
    ring(4)

    def wait_w(k):
        sender = lax.rem(f + F - k, F)
        w_copy(0, f, sender).wait_recv()
        w_copy(1, f, sender).wait_recv()

    w_copy(1, f, f).wait_recv()
    loop(1, F, wait_w)

    def part(t):
        if t == 0:
            acc[at(z, TB), :] = dot_t(dh[at(z, TB), :], w2[...])
            return
        for way in range(2):
            rows = at(ring_block(way, t), TB)
            cols = pl.ds(0, CR) if way == 0 else pl.ds(CR, D - CR)
            term = dot_t(dh[rows, cols], w2[:, cols])
            if t < NZ // 2 or (t == NZ // 2 and way == 0):
                acc[rows, :] = term
            else:
                acc[rows, :] += term

    def dconv_copy(block, half):
        rows = pl.ds(pl.multiple_of(half * HALF + block * TB, TB), TB)
        return remote(dcv.at[at(block, TB), :], dch.at[rows, :], x_s.at[block], x_r.at[block], f, pr)

    def dg_copy(n, peer_z, channel):
        return remote(
            dg.at[n, at(peer_z, TB), :], dgt.at[:, at(channel, CB)],
            dg_s.at[n, peer_z], dg_r.at[channel], f, xl * NZ + peer_z,
        )

    own_dg = [
        pltpu.make_async_copy(dg.at[n, at(z, TB), :], dgt.at[:, at(c, CB)], local.at[5 + n])
        for n, c in enumerate((r, pr))
    ]

    def finalize(block):
        rows = at(block, TB)
        for n in range(2):
            d = acc[rows, n * CB : (n + 1) * CB]
            gate = gmn[n, rows, :].astype(F32)
            conv = cmn[n, rows, :].astype(F32)
            gt[n * CB : (n + 1) * CB, rows] = (gate * conv).T.astype(BF)
            dg[n, rows, :] = (d * conv).astype(BF)
            dconv = (d * gate).astype(BF)
            if n == 0:
                dch[pl.ds(pl.multiple_of(xl * HALF + block * TB, TB), TB), :] = dconv
            else:
                dcv[rows, :] = dconv
        dconv_copy(block, xl).start()

    def wait_gate(k):
        sender = lax.rem(z + NZ - k, NZ)
        gate_copy(0, z, sender).wait_recv()
        gate_copy(1, z, sender).wait_recv()

    def step_done(t):
        part(t)
        if t == 0:
            finalize(z)
        elif t == NZ // 2:
            finalize(ring_block(0, t))
        elif t > NZ // 2:
            finalize(ring_block(0, t))
            finalize(ring_block(1, t))

    for t in range(1, min(4, NZ)):
        part(t)
    loop(1, NZ, wait_gate)
    conv_copy.wait_recv()
    step_done(0)
    if NZ <= 4:
        for t in range(NZ // 2, NZ):
            finalize(ring_block(0, t))
            if t > NZ // 2:
                finalize(ring_block(1, t))
    ring(5)
    def send_dg(k):
        peer = lax.rem(z + k, NZ)
        dg_copy(0, peer, r).start()
        dg_copy(1, peer, pr).start()

    for t in range(4, NZ):
        if t == NZ - 1:
            loop(2, NZ - 1, send_dg)
        step_done(t)
        ring(t + 2)
    if NZ <= 4:
        loop(2, NZ - 1, send_dg)
    send_dg(1)
    if NZ > 2:
        send_dg(NZ - 1)
    for copy in own_dg:
        copy.start()

    def gw_partial(cols):
        return dot(gt[...], dh[:, at(cols, DB)])

    def gwx_copy(j):
        return remote(gwx.at[j], gwy.at[j], gwx_s.at[j], gwx_r.at[j], twin, r)

    def gwx_step(k):
        j = lax.rem(chip + k, FC)
        gwx[j] = gw_partial(2 * j + 1 - core).astype(BF)
        gwx_copy(j).start()

    loop(0, FC, gwx_step)

    def gw_copy(n, peer, sender):
        return remote(gws.at[peer, n], gwr.at[n, sender], gw_s.at[n, peer], gw_r.at[n, sender], 2 * peer + core, (r, pr)[n])

    def gw_step(j):
        total = gw_partial(2 * j + core)
        gwx_copy(j).wait_recv()
        piece = (total + gwy[j].astype(F32)).astype(BF)
        gws[j, 0] = piece[:CB]
        gws[j, 1] = piece[CB:]
        gw_copy(1, j, chip).start()

    def gw_send_step(k):
        j = lax.rem(chip + k, FC)
        gw_step(j)
        gw_copy(0, j, chip).start()

    loop(1, FC, gw_send_step)
    gw_step(chip)

    loop(0, NZ, lambda k: dconv_copy(k, 1 - xl).wait_recv())
    loop(0, CHUNKS, plane_step(dch))
    rows_fwd(dsp)
    rows_inv(dsp, fsp, True)

    def dm_copy(peer, sender):
        return remote(dms.at[at(peer, TB), :], dmt.at[:, at(sender, CB)], dm_s.at[peer], dm_r.at[sender], f, peer)

    def dm_send(peer):
        @pl.when(peer != r)
        def _():
            dm_copy(peer, r).start()

    def dmixed_step(k):
        chunk = lax.rem(lax.div(r * TB, CH) + 1 + k, CHUNKS)
        dms[at(chunk, CH), :] = columns_inv(chunk).astype(BF)
        for n in range(CH // TB):
            dm_send(chunk * (CH // TB) + n)

    loop(0, CHUNKS, dmixed_step)
    own_dm = pltpu.make_async_copy(dms.at[at(r, TB), :], dmt.at[:, at(r, CB)], local.at[7])
    own_dm.start()

    rows_inv(dsp, msp, True)

    def gf_step(k):
        gff[at(k, CH), :] = columns_inv(k)

    loop(0, CHUNKS, gf_step)

    def gfx_copy(j):
        return remote(gfx.at[j], gfy.at[j], gfx_s.at[j], gfx_r.at[j], twin, r)

    def gfx_step(j):
        gfx[j] = gff[at(2 * j + 1 - core, PB), :].astype(BF)
        gfx_copy(j).start()

    loop(0, FC, gfx_step)

    def gf_copy(peer, sender):
        return remote(gfs.at[peer], gfr.at[sender], gf_s.at[peer], gf_r.at[sender], 2 * peer + core, r)

    def gf_sum(j):
        gfx_copy(j).wait_recv()
        gfs[j] = (gff[at(2 * j + core, PB), :] + gfy[j].astype(F32)).astype(BF)

    def gf_send_step(k):
        j = lax.rem(chip + k, FC)
        gf_sum(j)
        gf_copy(j, chip).start()

    loop(1, FC, gf_send_step)
    gf_sum(chip)

    gw_out[...] = gws[chip, 0].astype(F32)

    def gw_add(n, sender):
        gw_copy(n, chip, sender).wait_recv()
        gw_out[...] += gwr[n, sender].astype(F32)

    def gw_arrive(k):
        sender = lax.rem(chip + FC - k, FC)
        gw_add(0, sender)
        gw_add(1, sender)

    loop(1, FC, gw_arrive)
    gw_add(1, chip)
    gw_out[...] = gw_out[...] * (1.0 / F)

    gfr[chip] = gfs[chip]
    loop(1, FC, lambda k: gf_copy(chip, lax.rem(chip + FC - k, FC)).wait_recv())
    total = gfr[0].astype(F32)
    for n in range(1, FC):
        total = total + gfr[n].astype(F32)
    gf_out[...] = total.T * (1.0 / F)

    for copy in own_dg:
        copy.wait()

    def dg_arrive(k):
        sender = lax.rem(z + NZ - k, NZ)
        dg_copy(0, z, xl * NZ + sender).wait_recv()
        dg_copy(1, z, (1 - xl) * NZ + sender).wait_recv()

    loop(1, NZ, dg_arrive)

    own_dm.wait()
    loop(1, R, lambda k: dm_copy(r, lax.rem(r + R - k, R)).wait_recv())

    for step in range(NZ - 1):
        for way in range(2):
            for sub in range(SUB):
                ring_copy(way, sub, step, ring_block(way, step)).wait_send()

    def row_sent(k):
        peer = lax.rem(r + k, R)
        mx_copy(peer, r).wait_send()
        dm_copy(peer, r).wait_send()

    loop(1, R, row_sent)

    def z_sent(k):
        peer = lax.rem(z + k, NZ)
        for n in range(2):
            gate_copy(n, peer, z).wait_send()
            dg_copy(n, peer, (r, pr)[n]).wait_send()

    loop(1, NZ, z_sent)
    loop(0, NZ, lambda k: dconv_copy(k, xl).wait_send())

    def plane_sent(k):
        peer = lax.rem(f + k, F)
        for n in range(2):
            w_copy(n, peer, f).wait_send()

    loop(1, F, plane_sent)

    def chip_sent(k):
        peer = lax.rem(chip + k, FC)
        gw_copy(0, peer, chip).wait_send()
        gf_copy(peer, chip).wait_send()

    loop(1, FC, chip_sent)

    def twin_sent(j):
        gw_copy(1, j, chip).wait_send()
        gwx_copy(j).wait_send()
        gfx_copy(j).wait_send()

    loop(0, FC, twin_sent)
    w_copy(1, f, f).wait_send()
    conv_copy.wait_send()


def finish(value, gate_a, dmixed, dgate, gw, gf, out, gw_out, gf_out):
    D = dmixed.shape[1]
    d = dmixed[...].astype(F32)
    out[:, :D] = (d * gate_a[...].astype(F32)).astype(BF)
    out[:, D : 2 * D] = (d * value[...].astype(F32)).astype(BF)
    out[:, 2 * D :] = dgate[...]

    @pl.when(pl.program_id(0) == 0)
    def _():
        gw_out[...] = gw[...]
        gf_out[...] = gf[...]


def local(R, F, proj, dout, filt, w):
    proj, dout = proj.reshape(proj.shape[1:]), dout.reshape(dout.shape[1:])
    D = dout.shape[1]
    NZ = R // 2
    TB, CB, DB, PB = POS // R, D // R, D // F, POS // F
    CR = D * RIGHT // 16 // (128 * SUB) * (128 * SUB)
    tables = [jnp.asarray(t) for t in build_tables()]
    vmem = pl.BlockSpec(memory_space=pltpu.VMEM)
    hbm = pl.BlockSpec(memory_space=pl.ANY)
    dma = pltpu.SemaphoreType.DMA
    spectrum = pltpu.VMEM((LC + 2, LR, CB), F32)
    grads = pl.pallas_call(
        functools.partial(kernel, R, F, D, CR),
        out_shape=(
            jax.ShapeDtypeStruct((TB, D), BF),
            jax.ShapeDtypeStruct((TB, D), BF),
            jax.ShapeDtypeStruct((CB, DB), F32),
            jax.ShapeDtypeStruct((CB, PB), F32),
        ),
        in_specs=[
            hbm, hbm, hbm, hbm,
        ] + [hbm] * len(tables),
        out_specs=(hbm, hbm, vmem, vmem),
        scratch_shapes=[
            pltpu.VMEM((CB, POS), F32),
        ] + [pltpu.VMEM(t.shape, BF) for t in tables] + [
            pltpu.VMEM((TB, D), BF), pltpu.VMEM((TB, D), BF),
            pltpu.VMEM((TB, D), BF),
            pltpu.VMEM((POS, CB), BF),
            pltpu.VMEM((2, HALF, CB), BF),
            pltpu.VMEM((2, HALF, CB), BF),
            pltpu.VMEM((HALF, CB), BF),
            pltpu.VMEM((HALF, D), BF),
            pltpu.VMEM((2 * CB, D), BF),
            spectrum, spectrum, spectrum,
            pltpu.VMEM((LC, LR, CB), F32),
            pltpu.VMEM((HALF, 2 * CB), F32),
            pltpu.VMEM((2 * CB, HALF), BF),
            pltpu.VMEM((HALF, CB), BF),
            pltpu.VMEM((POS, CB), BF),
            pltpu.VMEM((2, HALF, CB), BF),
            pltpu.VMEM((POS, CB), BF),
            pltpu.VMEM((F // 2, 2 * CB, DB), BF), pltpu.VMEM((F // 2, 2 * CB, DB), BF),
            pltpu.VMEM((F // 2, 2, CB, DB), BF), pltpu.VMEM((2, F // 2, CB, DB), BF),
            pltpu.VMEM((POS, CB), F32),
            pltpu.VMEM((F // 2, PB, CB), BF), pltpu.VMEM((F // 2, PB, CB), BF),
            pltpu.VMEM((F // 2, PB, CB), BF), pltpu.VMEM((F // 2, PB, CB), BF),
            dma((23,)),
            dma((2 * SUB, NZ)), dma((2 * SUB, NZ)),
            dma((R,)), dma((R,)),
            dma((2, NZ)), dma((2, NZ)),
            dma((2, F)), dma((2, F)),
            dma((NZ + 1,)), dma((NZ + 1,)),
            dma((2, NZ)), dma((R,)),
            dma((R,)), dma((R,)),
            dma((F // 2,)), dma((F // 2,)), dma((2, F // 2)), dma((2, F // 2)),
            dma((F // 2,)), dma((F // 2,)), dma((F // 2,)), dma((F // 2,)),
        ],
        compiler_params=pltpu.CompilerParams(
            collective_id=0, has_side_effects=True, vmem_limit_bytes=62 * 1024 * 1024
        ),
    )(proj, dout, w, filt, *tables)
    dmixed, dgate, gw, gf = grads
    rows = TB // 2
    whole = lambda *shape: pl.BlockSpec(shape, lambda i: (0, 0))
    grad_proj, gw, gf = pl.pallas_call(
        finish,
        grid=(TB // rows,),
        out_shape=(
            jax.ShapeDtypeStruct((TB, 3 * D), BF),
            jax.ShapeDtypeStruct((CB, DB), F32),
            jax.ShapeDtypeStruct((CB, PB), F32),
        ),
        in_specs=[
            pl.BlockSpec((rows, D), lambda i: (i, 0)),
            pl.BlockSpec((rows, D), lambda i: (i, 1)),
            pl.BlockSpec((rows, D), lambda i: (i, 0)),
            pl.BlockSpec((rows, D), lambda i: (i, 0)),
            whole(CB, DB),
            whole(CB, PB),
        ],
        out_specs=(pl.BlockSpec((rows, 3 * D), lambda i: (i, 0)), whole(CB, DB), whole(CB, PB)),
    )(proj, proj, dmixed, dgate, gw, gf)
    return grad_proj[None], gw, gf


def solution(mesh):
    placed = (P("frame", "row", None), P("frame", "row", None), P("row", None), P("row", "frame"))
    return jax.shard_map(
        functools.partial(local, mesh.shape["row"], mesh.shape["frame"]),
        mesh=mesh,
        in_specs=placed,
        out_specs=(P("frame", "row", None), P("row", "frame"), P("row", "frame")),
        check_vma=False,
    )
```

```python
import functools

import jax
import jax.numpy as jnp
import ml_dtypes
import numpy as np
from jax import lax
from jax.experimental import pallas as pl
from jax.experimental.pallas import tpu as pltpu
from jax.sharding import PartitionSpec as P

LR = 64
LC = 32
POS = LR * LC
HALF = POS // 2
RIGHT = 8
SUB = 2
ROWS = 5
COLS = 4
G = 8
MESH = pl.DeviceIdType.MESH
BF = jnp.bfloat16
F32 = jnp.float32


def split_table(table):
    high = table.astype(ml_dtypes.bfloat16)
    low = (table - high.astype(np.float64)).astype(ml_dtypes.bfloat16)
    return high, low


def build_tables():
    j = np.arange(LC)
    fwd = np.zeros((LC, LC))
    inv = np.zeros((LC, LC))
    fwd[0], inv[:, 0] = 1.0, 1.0
    fwd[1] = np.cos(np.pi * j)
    inv[:, 1] = np.cos(np.pi * j)
    for l in range(1, LC // 2):
        angle = 2 * np.pi * ((j * l) % LC) / LC
        fwd[2 * l], fwd[2 * l + 1] = np.cos(angle), -np.sin(angle)
        inv[:, 2 * l], inv[:, 2 * l + 1] = 2 * np.cos(angle), -2 * np.sin(angle)
    inv = inv / POS
    eye = np.eye(G)
    col_fwd = np.einsum("qj,ab->qabj", fwd, eye).reshape(G * LC, G * LC)
    col_inv = np.einsum("jq,ab->ajqb", inv, eye).reshape(G * LC, G * LC)
    i = np.arange(LR)
    angle = 2 * np.pi * ((i[:, None] * i[None, :]) % LR) / LR
    c, s = np.cos(angle), np.sin(angle)
    o = np.zeros_like(c)
    row_fwd = np.block([[c, s], [-s, c]])
    row_inv = np.block([[c, -s], [s, c]])
    edge_fwd = np.block([[c, o], [-s, o], [o, c], [o, -s]])
    edge_inv = np.block([[c, -s, o, o], [o, o, c, -s]])
    out = []
    for table in (col_fwd, row_fwd, edge_fwd, row_inv, edge_inv, col_inv):
        out.extend(split_table(table))
    return tuple(out)


def split(x):
    high = x.astype(BF)
    return high, (x - high.astype(F32)).astype(BF)


def dot(a, b):
    return jnp.dot(a, b, preferred_element_type=F32)


def dot_t(a, b):
    return lax.dot_general(a, b, (((1,), (1,)), ((), ())), preferred_element_type=F32)


def dot3(high, low, x, product=dot):
    x_high, x_low = split(x)
    return product(high, x_high) + product(high, x_low) + product(low, x_high)


def kernel(
    R, F, D, CR,
    proj, dout, w, filt_hbm, t0, t1, t2, t3, t4, t5, t6, t7, t8, t9, t10, t11,
    dmt, dgt, gw_out, gf_out,
    filt, a1h, a1l, a2h, a2l, azh, azl, b2h, b2l, bzh, bzl, b1h, b1l,
    value, gate_a, mx, mch, gmn, cmn, cvo, dh, w2, fsp, msp, dsp, tmp, acc, gt, dcv, dch, dg, dms,
    gwx, gwy, gws, gwr, gwp, gwq, gff, gfx, gfy, gfs, gfr,
    local, ring_s, ring_r, mx_s, mx_r, gate_s, gate_r, w_s, w_r, x_s, x_r, dg_s, dg_r, dm_s, dm_r,
    gwx_s, gwx_r, gw_s, gw_r, gwz_s, gwz_r, gfx_s, gfx_r, gf_s, gf_r,
):
    NZ = R // 2
    TB, CB, DB, PB = POS // R, D // R, D // F, POS // F
    f, r = lax.axis_index("frame"), lax.axis_index("row")
    xl, z = lax.div(r, NZ), lax.rem(r, NZ)
    pr = (1 - xl) * NZ + z
    right = xl * NZ + lax.rem(z + 1, NZ)
    left = xl * NZ + lax.rem(z + NZ - 1, NZ)
    FC = F // 2
    chip, core = lax.div(f, 2), lax.rem(f, 2)
    twin = f + 1 - 2 * core
    NX = 2 if F >= 8 else 1
    NY = FC // NX
    xh, y = lax.div(chip, NY), lax.rem(chip, NY)

    def at(index, size):
        return pl.ds(pl.multiple_of(index * size, size), size)

    def remote(src, dst, send, recv, frame, row):
        return pltpu.make_async_remote_copy(
            src_ref=src, dst_ref=dst, send_sem=send, recv_sem=recv,
            device_id={"frame": frame, "row": row}, device_id_type=MESH,
        )

    def loop(start, stop, step, unroll=1):
        def body(k, carry):
            step(k)
            return carry

        lax.fori_loop(start, stop, body, 0, unroll=unroll)

    barrier = pltpu.get_barrier_semaphore()

    def greet(frame, row):
        pl.semaphore_signal(barrier, inc=1, device_id={"frame": frame, "row": row}, device_id_type=MESH)

    loop(1, R, lambda k: greet(f, lax.rem(r + k, R)))

    def greet_plane(k):
        greet(lax.rem(f + k, F), r)
        greet(lax.rem(f + k, F), pr)

    loop(1, F, greet_plane)

    own_dout = pltpu.make_async_copy(dout, dh.at[at(z, TB), :], local.at[0])
    own_w = pltpu.make_async_copy(w, w2.at[pl.ds(0, CB), at(f, DB)], local.at[1])
    own_gate = [
        pltpu.make_async_copy(proj.at[:, at(2 * R + c, CB)], gmn.at[n, at(z, TB), :], local.at[2 + n])
        for n, c in enumerate((r, pr))
    ]
    own_value = pltpu.make_async_copy(proj.at[:, pl.ds(0, D)], value, local.at[8])
    own_a = pltpu.make_async_copy(proj.at[:, pl.ds(D, D)], gate_a, local.at[9])
    own_value.start()
    own_a.start()
    own_dout.start()
    own_w.start()
    for copy in own_gate:
        copy.start()
    own_tables = [
        pltpu.make_async_copy(pair[0], pair[1], local.at[10 + n])
        for n, pair in enumerate(
            zip(
                (filt_hbm, t0, t1, t2, t3, t4, t5, t6, t7, t8, t9, t10, t11),
                (filt, a1h, a1l, a2h, a2l, azh, azl, b2h, b2l, bzh, bzl, b1h, b1l),
            )
        )
    ]
    for copy in own_tables:
        copy.start()

    own_value.wait()
    own_a.wait()
    mx[...] = (value[...].astype(F32) * gate_a[...].astype(F32)).astype(BF)
    own_mx = pltpu.make_async_copy(mx.at[:, at(r, CB)], mch.at[at(r, TB), :], local.at[4])
    own_mx.start()
    pl.semaphore_wait(barrier, (R - 1) + 2 * (F - 1))

    def ring_part(way, sub):
        width = (CR if way == 0 else D - CR) // SUB
        return pl.ds((0 if way == 0 else CR) + sub * width, width)

    def ring_copy(way, sub, step, block):
        place = dh.at[at(block, TB), ring_part(way, sub)]
        n = way * SUB + sub
        first = dout.at[:, ring_part(way, sub)] if step == 0 else place
        return remote(first, place, ring_s.at[n, step], ring_r.at[n, step], f, (right, left)[way])

    def ring_block(way, step):
        return lax.rem(z + NZ - step, NZ) if way == 0 else lax.rem(z + step, NZ)

    def ring(step):
        if step < NZ:
            for sub in range(SUB):
                for way in range(2):
                    if step > 0:
                        ring_copy(way, sub, step - 1, ring_block(way, step)).wait_recv()
                    if step < NZ - 1:
                        ring_copy(way, sub, step, ring_block(way, step)).start()

    def mx_copy(peer, sender):
        return remote(mx.at[:, at(peer, CB)], mch.at[at(sender, TB), :], mx_s.at[peer], mx_r.at[sender], f, peer)

    def gate_copy(n, peer_z, sender_z):
        c = (xl if n == 0 else 1 - xl) * NZ + peer_z
        return remote(
            proj.at[:, at(2 * R + c, CB)], gmn.at[n, at(sender_z, TB), :],
            gate_s.at[n, peer_z], gate_r.at[n, sender_z], f, xl * NZ + peer_z,
        )

    def w_copy(n, peer, sender):
        return remote(
            w, w2.at[pl.ds(n * CB, CB), at(sender, DB)], w_s.at[n, peer], w_r.at[n, sender], peer, (r, pr)[n]
        )

    def send_w(k):
        peer = lax.rem(f + k, F)
        w_copy(0, peer, f).start()
        w_copy(1, peer, f).start()

    ring(0)

    def send_mx(k):
        peer = lax.rem(r + k, R)
        mx_copy(peer, r).start()

    loop(1, R, send_mx)

    def send_gate(k):
        peer = lax.rem(z + k, NZ)
        gate_copy(0, peer, z).start()
        gate_copy(1, peer, z).start()

    loop(1, NZ, send_gate)
    w_copy(1, f, f).start()
    loop(1, F, send_w)

    def columns(k, part):
        tmp[:, at(k, G), :] = part.reshape(LC, G, CB)

    def pair(ref, index):
        return ref[pl.ds(index, 2)].reshape(2 * LR, CB)

    def rows_fwd(dst):
        edge = dot3(azh[...], azl[...], pair(tmp, 0)).reshape(4, LR, CB)
        dst[0:2] = edge[0:2]
        dst[LC : LC + 2] = edge[2:4]

        def step(l):
            dst[pl.ds(2 * l, 2)] = dot3(a2h[...], a2l[...], pair(tmp, 2 * l)).reshape(2, LR, CB)

        loop(1, LC // 2, step, ROWS)

    def multiply(a, b, conjugate):
        are, aim, bre, bim = a[0], a[1], b[0], b[1]
        if conjugate:
            both = are * bre + aim * bim, aim * bre - are * bim
        else:
            both = are * bre - aim * bim, are * bim + aim * bre
        return jnp.concatenate(both, axis=0)

    def rows_product(a, b, conjugate, forward):
        if forward:
            edge = dot3(azh[...], azl[...], pair(tmp, 0)).reshape(4, LR, CB)
            a[0:2] = edge[0:2]
            a[LC : LC + 2] = edge[2:4]
        else:
            edge = jnp.concatenate((a[0:2], a[LC : LC + 2]), axis=0)
        edge = jnp.concatenate((multiply(edge[0:2], b[0:2], conjugate), multiply(edge[2:4], b[LC : LC + 2], conjugate)), axis=0)
        tmp[0:2] = dot3(bzh[...], bzl[...], edge).reshape(2, LR, CB)

        def step(l):
            place = pl.ds(2 * l, 2)
            if forward:
                spectrum = dot3(a2h[...], a2l[...], pair(tmp, 2 * l)).reshape(2, LR, CB)
                a[place] = spectrum
            else:
                spectrum = a[place]
            tmp[place] = dot3(b2h[...], b2l[...], multiply(spectrum, b[place], conjugate)).reshape(2, LR, CB)

        loop(1, LC // 2, step, ROWS)

    def columns_inv(k):
        return dot3(b1h[...], b1l[...], tmp[:, at(k, G), :].reshape(G * LC, CB))

    CH = G * LC
    CHUNKS = POS // CH

    def filt_step(k):
        columns(k, dot3(a1h[...], a1l[...], filt[:, at(k, CH)], dot_t))

    for copy in own_tables:
        copy.wait()
    loop(0, CHUNKS, filt_step, COLS)
    ring(1)
    rows_fwd(fsp)

    own_mx.wait()

    def wait_mx(k):
        sender = lax.rem(r + R - k, R)
        mx_copy(r, sender).wait_recv()

    loop(1, R, wait_mx)
    ring(2)

    def plane_step(src):
        def step(k):
            x = src[at(k, CH), :]
            columns(k, dot(a1h[...], x) + dot(a1l[...], x))

        return step

    loop(0, CHUNKS, plane_step(mch), COLS)
    ring(3)
    rows_product(msp, fsp, False, True)

    def conv_step(k):
        cmn[0, at(k, CH), :] = columns_inv(xl * (CHUNKS // 2) + k).astype(BF)
        cvo[at(k, CH), :] = columns_inv((1 - xl) * (CHUNKS // 2) + k).astype(BF)

    loop(0, CHUNKS // 2, conv_step, COLS // 2)
    conv_copy = remote(cvo, cmn.at[1], x_s.at[NZ], x_r.at[NZ], f, pr)
    conv_copy.start()
    for copy in own_gate:
        copy.wait()
    own_w.wait()
    own_dout.wait()
    ring(4)

    def wait_w(k):
        sender = lax.rem(f + F - k, F)
        w_copy(0, f, sender).wait_recv()
        w_copy(1, f, sender).wait_recv()

    w_copy(1, f, f).wait_recv()
    loop(1, F, wait_w)

    def part(t):
        if t == 0:
            acc[at(z, TB), :] = dot_t(dh[at(z, TB), :], w2[...])
            return
        for way in range(2):
            rows = at(ring_block(way, t), TB)
            cols = pl.ds(0, CR) if way == 0 else pl.ds(CR, D - CR)
            term = dot_t(dh[rows, cols], w2[:, cols])
            if t < NZ // 2 or (t == NZ // 2 and way == 0):
                acc[rows, :] = term
            else:
                acc[rows, :] += term

    def dconv_copy(block, half):
        rows = pl.ds(pl.multiple_of(half * HALF + block * TB, TB), TB)
        return remote(dcv.at[at(block, TB), :], dch.at[rows, :], x_s.at[block], x_r.at[block], f, pr)

    def dg_copy(n, peer_z, channel):
        return remote(
            dg.at[n, at(peer_z, TB), :], dgt.at[:, at(channel, CB)],
            dg_s.at[n, peer_z], dg_r.at[channel], f, xl * NZ + peer_z,
        )

    own_dg = [
        pltpu.make_async_copy(dg.at[n, at(z, TB), :], dgt.at[:, at(c, CB)], local.at[5 + n])
        for n, c in enumerate((r, pr))
    ]

    def finalize(block):
        rows = at(block, TB)
        for n in range(2):
            d = acc[rows, n * CB : (n + 1) * CB]
            gate = gmn[n, rows, :].astype(F32)
            conv = cmn[n, rows, :].astype(F32)
            gt[n * CB : (n + 1) * CB, rows] = (gate * conv).T.astype(BF)
            dg[n, rows, :] = (d * conv).astype(BF)
            dconv = (d * gate).astype(BF)
            if n == 0:
                dch[pl.ds(pl.multiple_of(xl * HALF + block * TB, TB), TB), :] = dconv
            else:
                dcv[rows, :] = dconv
        dconv_copy(block, xl).start()

    def wait_gate(k):
        sender = lax.rem(z + NZ - k, NZ)
        gate_copy(0, z, sender).wait_recv()
        gate_copy(1, z, sender).wait_recv()

    def step_done(t):
        part(t)
        if t == 0:
            finalize(z)
        elif t == NZ // 2:
            finalize(ring_block(0, t))
        elif t > NZ // 2:
            finalize(ring_block(0, t))
            finalize(ring_block(1, t))

    for t in range(1, min(4, NZ)):
        part(t)
    loop(1, NZ, wait_gate)
    conv_copy.wait_recv()
    step_done(0)
    if NZ <= 4:
        for t in range(NZ // 2, NZ):
            finalize(ring_block(0, t))
            if t > NZ // 2:
                finalize(ring_block(1, t))
    ring(5)
    def send_dg(k):
        peer = lax.rem(z + k, NZ)
        dg_copy(0, peer, r).start()
        dg_copy(1, peer, pr).start()

    for t in range(4, NZ):
        if t == NZ - 1:
            loop(2, NZ - 1, send_dg)
        step_done(t)
        ring(t + 2)
    if NZ <= 4:
        loop(2, NZ - 1, send_dg)
    send_dg(1)
    if NZ > 2:
        send_dg(NZ - 1)
    for copy in own_dg:
        copy.start()

    def gw_partial(cols):
        return dot(gt[...], dh[:, at(cols, DB)])

    def gwx_copy(j):
        return remote(gwx.at[j], gwy.at[j], gwx_s.at[j], gwx_r.at[j], twin, r)

    def gwx_step(k):
        j = lax.rem(chip + k, FC)
        gwx[j] = gw_partial(2 * j + 1 - core).astype(BF)
        gwx_copy(j).start()

    loop(0, FC, gwx_step)

    def gwy_copy(h, peer, sender):
        return remote(gws.at[peer, h], gwr.at[sender, h], gw_s.at[h, peer], gw_r.at[h, sender], (xh * NY + peer) * 2 + core, r)

    def gw_step(peer):
        for h in range(NX):
            j = h * NY + peer
            total = gw_partial(2 * j + core)
            gwx_copy(j).wait_recv()
            gws[peer, h] = (total + gwy[j].astype(F32)).astype(BF)

    def gw_send_step(k):
        peer = lax.rem(y + k, NY)
        gw_step(peer)
        for h in range(NX):
            gwy_copy(h, peer, y).start()

    loop(1, NY, gw_send_step)
    gw_step(y)

    loop(0, NZ, lambda k: dconv_copy(k, 1 - xl).wait_recv())
    loop(0, CHUNKS, plane_step(dch), COLS)
    rows_product(dsp, fsp, True, True)

    def dm_copy(peer, sender):
        return remote(dms.at[at(peer, TB), :], dmt.at[:, at(sender, CB)], dm_s.at[peer], dm_r.at[sender], f, peer)

    def dm_send(peer):
        @pl.when(peer != r)
        def _():
            dm_copy(peer, r).start()

    def dmixed_step(k):
        chunk = lax.rem(lax.div(r * TB, CH) + 1 + k, CHUNKS)
        dms[at(chunk, CH), :] = columns_inv(chunk).astype(BF)
        for n in range(CH // TB):
            dm_send(chunk * (CH // TB) + n)

    loop(0, CHUNKS, dmixed_step, COLS)
    own_dm = pltpu.make_async_copy(dms.at[at(r, TB), :], dmt.at[:, at(r, CB)], local.at[7])
    own_dm.start()

    def gwz_copy(h, n):
        return remote(gwp.at[h, n], gwq.at[h, n], gwz_s.at[h, n], gwz_r.at[h, n], (lax.rem(xh + h, NX) * NY + y) * 2 + core, (r, pr)[n])

    def gw_over_y():
        for h in range(NX):
            block = lax.rem(xh + h, NX)
            total = gws[y, block].astype(F32)
            for k in range(1, NY):
                sender = lax.rem(y + k, NY)
                gwy_copy(block, y, sender).wait_recv()
                total = total + gwr[sender, block].astype(F32)
            if h == 0:
                gw_out[...] = total[:CB]
            else:
                gwp[h, 0] = total[:CB].astype(BF)
                gwz_copy(h, 0).start()
            gwp[h, 1] = total[CB:].astype(BF)
            gwz_copy(h, 1).start()

    rows_product(dsp, msp, True, False)

    def gf_step(k):
        gff[at(k, CH), :] = columns_inv(k)

    loop(0, CHUNKS, gf_step, COLS)

    def gfx_copy(j):
        return remote(gfx.at[j], gfy.at[j], gfx_s.at[j], gfx_r.at[j], twin, r)

    def gfx_step(j):
        gfx[j] = gff[at(2 * j + 1 - core, PB), :].astype(BF)
        gfx_copy(j).start()

    loop(0, FC, gfx_step)

    def gf_copy(peer, sender):
        return remote(gfs.at[peer], gfr.at[sender], gf_s.at[peer], gf_r.at[sender], 2 * peer + core, r)

    def gf_sum(j):
        gfx_copy(j).wait_recv()
        gfs[j] = (gff[at(2 * j + core, PB), :] + gfy[j].astype(F32)).astype(BF)

    def gf_send_step(k):
        j = lax.rem(chip + k, FC)
        gf_sum(j)
        gf_copy(j, chip).start()

    loop(1, FC, gf_send_step)
    gf_sum(chip)
    gw_over_y()

    gfr[chip] = gfs[chip]
    loop(1, FC, lambda k: gf_copy(chip, lax.rem(chip + FC - k, FC)).wait_recv())
    total = gfr[0].astype(F32)
    for n in range(1, FC):
        total = total + gfr[n].astype(F32)
    gf_out[...] = total.T * (1.0 / F)

    total = gw_out[...]
    for h in range(NX):
        for n in range(2):
            if h + n > 0:
                gwz_copy(h, n).wait_recv()
                total = total + gwq[h, n].astype(F32)
    gw_out[...] = total * (1.0 / F)

    for copy in own_dg:
        copy.wait()

    def dg_arrive(k):
        sender = lax.rem(z + NZ - k, NZ)
        dg_copy(0, z, xl * NZ + sender).wait_recv()
        dg_copy(1, z, (1 - xl) * NZ + sender).wait_recv()

    loop(1, NZ, dg_arrive)

    own_dm.wait()
    loop(1, R, lambda k: dm_copy(r, lax.rem(r + R - k, R)).wait_recv())

    for step in range(NZ - 1):
        for way in range(2):
            for sub in range(SUB):
                ring_copy(way, sub, step, ring_block(way, step)).wait_send()

    def row_sent(k):
        peer = lax.rem(r + k, R)
        mx_copy(peer, r).wait_send()
        dm_copy(peer, r).wait_send()

    loop(1, R, row_sent)

    def z_sent(k):
        peer = lax.rem(z + k, NZ)
        for n in range(2):
            gate_copy(n, peer, z).wait_send()
            dg_copy(n, peer, (r, pr)[n]).wait_send()

    loop(1, NZ, z_sent)
    loop(0, NZ, lambda k: dconv_copy(k, xl).wait_send())

    def plane_sent(k):
        peer = lax.rem(f + k, F)
        for n in range(2):
            w_copy(n, peer, f).wait_send()

    loop(1, F, plane_sent)

    def chip_sent(k):
        peer = lax.rem(chip + k, FC)
        gf_copy(peer, chip).wait_send()

    loop(1, FC, chip_sent)

    def twin_sent(j):
        gwx_copy(j).wait_send()
        gfx_copy(j).wait_send()

    loop(0, FC, twin_sent)

    def y_sent(k):
        for h in range(NX):
            gwy_copy(h, lax.rem(y + k, NY), y).wait_send()

    loop(1, NY, y_sent)
    for h in range(NX):
        for n in range(2):
            if h + n > 0:
                gwz_copy(h, n).wait_send()
    w_copy(1, f, f).wait_send()
    conv_copy.wait_send()


def finish(value, gate_a, dmixed, dgate, gw, gf, out, gw_out, gf_out):
    D = dmixed.shape[1]
    d = dmixed[...].astype(F32)
    out[:, :D] = (d * gate_a[...].astype(F32)).astype(BF)
    out[:, D : 2 * D] = (d * value[...].astype(F32)).astype(BF)
    out[:, 2 * D :] = dgate[...]

    @pl.when(pl.program_id(0) == 0)
    def _():
        gw_out[...] = gw[...]
        gf_out[...] = gf[...]


def local(R, F, proj, dout, filt, w):
    proj, dout = proj.reshape(proj.shape[1:]), dout.reshape(dout.shape[1:])
    D = dout.shape[1]
    NZ = R // 2
    TB, CB, DB, PB = POS // R, D // R, D // F, POS // F
    CR = D * RIGHT // 16 // (128 * SUB) * (128 * SUB)
    NX = 2 if F >= 8 else 1
    NY = F // 2 // NX
    tables = [jnp.asarray(t) for t in build_tables()]
    vmem = pl.BlockSpec(memory_space=pltpu.VMEM)
    hbm = pl.BlockSpec(memory_space=pl.ANY)
    dma = pltpu.SemaphoreType.DMA
    spectrum = pltpu.VMEM((LC + 2, LR, CB), F32)
    grads = pl.pallas_call(
        functools.partial(kernel, R, F, D, CR),
        out_shape=(
            jax.ShapeDtypeStruct((TB, D), BF),
            jax.ShapeDtypeStruct((TB, D), BF),
            jax.ShapeDtypeStruct((CB, DB), F32),
            jax.ShapeDtypeStruct((CB, PB), F32),
        ),
        in_specs=[
            hbm, hbm, hbm, hbm,
        ] + [hbm] * len(tables),
        out_specs=(hbm, hbm, vmem, vmem),
        scratch_shapes=[
            pltpu.VMEM((CB, POS), F32),
        ] + [pltpu.VMEM(t.shape, BF) for t in tables] + [
            pltpu.VMEM((TB, D), BF), pltpu.VMEM((TB, D), BF),
            pltpu.VMEM((TB, D), BF),
            pltpu.VMEM((POS, CB), BF),
            pltpu.VMEM((2, HALF, CB), BF),
            pltpu.VMEM((2, HALF, CB), BF),
            pltpu.VMEM((HALF, CB), BF),
            pltpu.VMEM((HALF, D), BF),
            pltpu.VMEM((2 * CB, D), BF),
            spectrum, spectrum, spectrum,
            pltpu.VMEM((LC, LR, CB), F32),
            pltpu.VMEM((HALF, 2 * CB), F32),
            pltpu.VMEM((2 * CB, HALF), BF),
            pltpu.VMEM((HALF, CB), BF),
            pltpu.VMEM((POS, CB), BF),
            pltpu.VMEM((2, HALF, CB), BF),
            pltpu.VMEM((POS, CB), BF),
            pltpu.VMEM((F // 2, 2 * CB, DB), BF), pltpu.VMEM((F // 2, 2 * CB, DB), BF),
            pltpu.VMEM((NY, NX, 2 * CB, DB), BF), pltpu.VMEM((NY, NX, 2 * CB, DB), BF),
            pltpu.VMEM((NX, 2, CB, DB), BF), pltpu.VMEM((NX, 2, CB, DB), BF),
            pltpu.VMEM((POS, CB), F32),
            pltpu.VMEM((F // 2, PB, CB), BF), pltpu.VMEM((F // 2, PB, CB), BF),
            pltpu.VMEM((F // 2, PB, CB), BF), pltpu.VMEM((F // 2, PB, CB), BF),
            dma((23,)),
            dma((2 * SUB, NZ)), dma((2 * SUB, NZ)),
            dma((R,)), dma((R,)),
            dma((2, NZ)), dma((2, NZ)),
            dma((2, F)), dma((2, F)),
            dma((NZ + 1,)), dma((NZ + 1,)),
            dma((2, NZ)), dma((R,)),
            dma((R,)), dma((R,)),
            dma((F // 2,)), dma((F // 2,)), dma((NX, NY)), dma((NX, NY)),
            dma((NX, 2)), dma((NX, 2)),
            dma((F // 2,)), dma((F // 2,)), dma((F // 2,)), dma((F // 2,)),
        ],
        compiler_params=pltpu.CompilerParams(
            collective_id=0, has_side_effects=True, vmem_limit_bytes=62 * 1024 * 1024
        ),
    )(proj, dout, w, filt, *tables)
    dmixed, dgate, gw, gf = grads
    rows = TB // 2
    whole = lambda *shape: pl.BlockSpec(shape, lambda i: (0, 0))
    grad_proj, gw, gf = pl.pallas_call(
        finish,
        grid=(TB // rows,),
        out_shape=(
            jax.ShapeDtypeStruct((TB, 3 * D), BF),
            jax.ShapeDtypeStruct((CB, DB), F32),
            jax.ShapeDtypeStruct((CB, PB), F32),
        ),
        in_specs=[
            pl.BlockSpec((rows, D), lambda i: (i, 0)),
            pl.BlockSpec((rows, D), lambda i: (i, 1)),
            pl.BlockSpec((rows, D), lambda i: (i, 0)),
            pl.BlockSpec((rows, D), lambda i: (i, 0)),
            whole(CB, DB),
            whole(CB, PB),
        ],
        out_specs=(pl.BlockSpec((rows, 3 * D), lambda i: (i, 0)), whole(CB, DB), whole(CB, PB)),
    )(proj, proj, dmixed, dgate, gw, gf)
    return grad_proj[None], gw, gf


def solution(mesh):
    placed = (P("frame", "row", None), P("frame", "row", None), P("row", None), P("row", "frame"))
    return jax.shard_map(
        functools.partial(local, mesh.shape["row"], mesh.shape["frame"]),
        mesh=mesh,
        in_specs=placed,
        out_specs=(P("frame", "row", None), P("row", "frame"), P("row", "frame")),
        check_vma=False,
    )
```

```python
import functools

import jax
import jax.numpy as jnp
import ml_dtypes
import numpy as np
from jax import lax
from jax.experimental import pallas as pl
from jax.experimental.pallas import tpu as pltpu
from jax.sharding import PartitionSpec as P

LR = 64
LC = 32
POS = LR * LC
HALF = POS // 2
RIGHT = 8
SUB = 2
ROWS = 5
COLS = 4
G = 8
MESH = pl.DeviceIdType.MESH
BF = jnp.bfloat16
F32 = jnp.float32


def split_table(table):
    high = table.astype(ml_dtypes.bfloat16)
    low = (table - high.astype(np.float64)).astype(ml_dtypes.bfloat16)
    return high, low


def build_tables():
    j = np.arange(LC)
    fwd = np.zeros((LC, LC))
    inv = np.zeros((LC, LC))
    fwd[0], inv[:, 0] = 1.0, 1.0
    fwd[1] = np.cos(np.pi * j)
    inv[:, 1] = np.cos(np.pi * j)
    for l in range(1, LC // 2):
        angle = 2 * np.pi * ((j * l) % LC) / LC
        fwd[2 * l], fwd[2 * l + 1] = np.cos(angle), -np.sin(angle)
        inv[:, 2 * l], inv[:, 2 * l + 1] = 2 * np.cos(angle), -2 * np.sin(angle)
    inv = inv / POS
    eye = np.eye(G)
    col_fwd = np.einsum("qj,ab->qabj", fwd, eye).reshape(G * LC, G * LC)
    col_inv = np.einsum("jq,ab->ajqb", inv, eye).reshape(G * LC, G * LC)
    i = np.arange(LR)
    angle = 2 * np.pi * ((i[:, None] * i[None, :]) % LR) / LR
    c, s = np.cos(angle), np.sin(angle)
    o = np.zeros_like(c)
    row_fwd = np.block([[c, s], [-s, c]])
    row_inv = np.block([[c, -s], [s, c]])
    edge_fwd = np.block([[c, o], [-s, o], [o, c], [o, -s]])
    edge_inv = np.block([[c, -s, o, o], [o, o, c, -s]])
    out = []
    for table in (col_fwd, row_fwd, edge_fwd, row_inv, edge_inv, col_inv):
        out.extend(split_table(table))
    return tuple(out)


def split(x):
    high = x.astype(BF)
    return high, (x - high.astype(F32)).astype(BF)


def dot(a, b):
    return jnp.dot(a, b, preferred_element_type=F32)


def dot_t(a, b):
    return lax.dot_general(a, b, (((1,), (1,)), ((), ())), preferred_element_type=F32)


def dot3(high, low, x, product=dot):
    x_high, x_low = split(x)
    return product(high, x_high) + product(high, x_low) + product(low, x_high)


def kernel(
    R, F, D, CR,
    proj, dout, w, filt_hbm, t0, t1, t2, t3, t4, t5, t6, t7, t8, t9, t10, t11,
    dmt, dgt, gw_out, gf_out,
    filt, a1h, a1l, a2h, a2l, azh, azl, b2h, b2l, bzh, bzl, b1h, b1l,
    value, gate_a, mx, mch, gmn, cmn, cvo, dh, w2, fsp, msp, dsp, tmp, acc, gt, dcv, dch, dg, dms,
    gwx, gwy, gws, gwr, gwp, gwq, gff, gfx, gfy, gfs, gfr,
    local, ring_s, ring_r, mx_s, mx_r, gate_s, gate_r, w_s, w_r, x_s, x_r, dg_s, dg_r, dm_s, dm_r,
    gwx_s, gwx_r, gw_s, gw_r, gwz_s, gwz_r, gfx_s, gfx_r, gf_s, gf_r,
):
    NZ = R // 2
    TB, CB, DB, PB = POS // R, D // R, D // F, POS // F
    f, r = lax.axis_index("frame"), lax.axis_index("row")
    xl, z = lax.div(r, NZ), lax.rem(r, NZ)
    pr = (1 - xl) * NZ + z
    right = xl * NZ + lax.rem(z + 1, NZ)
    left = xl * NZ + lax.rem(z + NZ - 1, NZ)
    FC = F // 2
    chip, core = lax.div(f, 2), lax.rem(f, 2)
    twin = f + 1 - 2 * core
    NX = 2 if F >= 8 else 1
    NY = FC // NX
    xh, y = lax.div(chip, NY), lax.rem(chip, NY)

    def at(index, size):
        return pl.ds(pl.multiple_of(index * size, size), size)

    def remote(src, dst, send, recv, frame, row):
        return pltpu.make_async_remote_copy(
            src_ref=src, dst_ref=dst, send_sem=send, recv_sem=recv,
            device_id={"frame": frame, "row": row}, device_id_type=MESH,
        )

    def loop(start, stop, step, unroll=1):
        def body(k, carry):
            step(k)
            return carry

        lax.fori_loop(start, stop, body, 0, unroll=unroll)

    barrier = pltpu.get_barrier_semaphore()

    def greet(frame, row):
        pl.semaphore_signal(barrier, inc=1, device_id={"frame": frame, "row": row}, device_id_type=MESH)

    loop(1, R, lambda k: greet(f, lax.rem(r + k, R)))

    def greet_plane(k):
        greet(lax.rem(f + k, F), r)
        greet(lax.rem(f + k, F), pr)

    loop(1, F, greet_plane)

    own_dout = pltpu.make_async_copy(dout, dh.at[at(z, TB), :], local.at[0])
    own_w = pltpu.make_async_copy(w, w2.at[pl.ds(0, CB), at(f, DB)], local.at[1])
    own_gate = [
        pltpu.make_async_copy(proj.at[:, at(2 * R + c, CB)], gmn.at[n, at(z, TB), :], local.at[2 + n])
        for n, c in enumerate((r, pr))
    ]
    own_value = pltpu.make_async_copy(proj.at[:, pl.ds(0, D)], value, local.at[8])
    own_a = pltpu.make_async_copy(proj.at[:, pl.ds(D, D)], gate_a, local.at[9])
    own_value.start()
    own_a.start()
    own_dout.start()
    own_w.start()
    for copy in own_gate:
        copy.start()
    own_tables = [
        pltpu.make_async_copy(pair[0], pair[1], local.at[10 + n])
        for n, pair in enumerate(
            zip(
                (filt_hbm, t0, t1, t2, t3, t4, t5, t6, t7, t8, t9, t10, t11),
                (filt, a1h, a1l, a2h, a2l, azh, azl, b2h, b2l, bzh, bzl, b1h, b1l),
            )
        )
    ]
    for copy in own_tables:
        copy.start()

    own_value.wait()
    own_a.wait()
    mx[...] = (value[...].astype(F32) * gate_a[...].astype(F32)).astype(BF)
    own_mx = pltpu.make_async_copy(mx.at[:, at(r, CB)], mch.at[at(r, TB), :], local.at[4])
    own_mx.start()
    pl.semaphore_wait(barrier, (R - 1) + 2 * (F - 1))

    def ring_part(way, sub):
        width = (CR if way == 0 else D - CR) // SUB
        return pl.ds((0 if way == 0 else CR) + sub * width, width)

    def ring_copy(way, sub, step, block):
        place = dh.at[at(block, TB), ring_part(way, sub)]
        n = way * SUB + sub
        first = dout.at[:, ring_part(way, sub)] if step == 0 else place
        return remote(first, place, ring_s.at[n, step], ring_r.at[n, step], f, (right, left)[way])

    def ring_block(way, step):
        return lax.rem(z + NZ - step, NZ) if way == 0 else lax.rem(z + step, NZ)

    def ring(step):
        if step < NZ:
            for sub in range(SUB):
                for way in range(2):
                    if step > 0:
                        ring_copy(way, sub, step - 1, ring_block(way, step)).wait_recv()
                    if step < NZ - 1:
                        ring_copy(way, sub, step, ring_block(way, step)).start()

    def mx_copy(peer, sender):
        return remote(mx.at[:, at(peer, CB)], mch.at[at(sender, TB), :], mx_s.at[peer], mx_r.at[sender], f, peer)

    def gate_copy(n, peer_z, sender_z):
        c = (xl if n == 0 else 1 - xl) * NZ + peer_z
        return remote(
            proj.at[:, at(2 * R + c, CB)], gmn.at[n, at(sender_z, TB), :],
            gate_s.at[n, peer_z], gate_r.at[n, sender_z], f, xl * NZ + peer_z,
        )

    def w_copy(n, peer, sender):
        return remote(
            w, w2.at[pl.ds(n * CB, CB), at(sender, DB)], w_s.at[n, peer], w_r.at[n, sender], peer, (r, pr)[n]
        )

    def send_w(k):
        peer = lax.rem(f + k, F)
        w_copy(0, peer, f).start()
        w_copy(1, peer, f).start()

    ring(0)

    def send_mx(k):
        peer = lax.rem(r + k, R)
        mx_copy(peer, r).start()

    loop(1, R, send_mx)

    def send_gate(k):
        peer = lax.rem(z + k, NZ)
        gate_copy(0, peer, z).start()
        gate_copy(1, peer, z).start()

    loop(1, NZ, send_gate)
    w_copy(1, f, f).start()
    loop(1, F, send_w)

    def columns(k, part):
        tmp[:, at(k, G), :] = part.reshape(LC, G, CB)

    def pair(ref, index):
        return ref[pl.ds(index, 2)].reshape(2 * LR, CB)

    def rows_fwd(dst):
        edge = dot3(azh[...], azl[...], pair(tmp, 0)).reshape(4, LR, CB)
        dst[0:2] = edge[0:2]
        dst[LC : LC + 2] = edge[2:4]

        def step(l):
            dst[pl.ds(2 * l, 2)] = dot3(a2h[...], a2l[...], pair(tmp, 2 * l)).reshape(2, LR, CB)

        loop(1, LC // 2, step, ROWS)

    def multiply(a, b, conjugate):
        are, aim, bre, bim = a[0], a[1], b[0], b[1]
        if conjugate:
            both = are * bre + aim * bim, aim * bre - are * bim
        else:
            both = are * bre - aim * bim, are * bim + aim * bre
        return jnp.concatenate(both, axis=0)

    def rows_product(a, b, conjugate, forward):
        if forward:
            edge = dot3(azh[...], azl[...], pair(tmp, 0)).reshape(4, LR, CB)
            a[0:2] = edge[0:2]
            a[LC : LC + 2] = edge[2:4]
        else:
            edge = jnp.concatenate((a[0:2], a[LC : LC + 2]), axis=0)
        edge = jnp.concatenate((multiply(edge[0:2], b[0:2], conjugate), multiply(edge[2:4], b[LC : LC + 2], conjugate)), axis=0)
        tmp[0:2] = dot3(bzh[...], bzl[...], edge).reshape(2, LR, CB)

        def step(l):
            place = pl.ds(2 * l, 2)
            if forward:
                spectrum = dot3(a2h[...], a2l[...], pair(tmp, 2 * l)).reshape(2, LR, CB)
                a[place] = spectrum
            else:
                spectrum = a[place]
            tmp[place] = dot3(b2h[...], b2l[...], multiply(spectrum, b[place], conjugate)).reshape(2, LR, CB)

        loop(1, LC // 2, step, ROWS)

    def columns_inv(k):
        return dot3(b1h[...], b1l[...], tmp[:, at(k, G), :].reshape(G * LC, CB))

    CH = G * LC
    CHUNKS = POS // CH

    def filt_step(k):
        columns(k, dot3(a1h[...], a1l[...], filt[:, at(k, CH)], dot_t))

    for copy in own_tables:
        copy.wait()
    loop(0, CHUNKS, filt_step, COLS)
    ring(1)
    rows_fwd(fsp)

    own_mx.wait()

    def wait_mx(k):
        sender = lax.rem(r + R - k, R)
        mx_copy(r, sender).wait_recv()

    loop(1, R, wait_mx)
    ring(2)

    def plane_step(src):
        def step(k):
            x = src[at(k, CH), :]
            columns(k, dot(a1h[...], x) + dot(a1l[...], x))

        return step

    loop(0, CHUNKS, plane_step(mch), COLS)
    ring(3)
    rows_product(msp, fsp, False, True)

    def conv_step(k):
        cmn[0, at(k, CH), :] = columns_inv(xl * (CHUNKS // 2) + k).astype(BF)
        cvo[at(k, CH), :] = columns_inv((1 - xl) * (CHUNKS // 2) + k).astype(BF)

    loop(0, CHUNKS // 2, conv_step, COLS // 2)
    conv_copy = remote(cvo, cmn.at[1], x_s.at[NZ], x_r.at[NZ], f, pr)
    conv_copy.start()
    for copy in own_gate:
        copy.wait()
    own_w.wait()
    own_dout.wait()
    ring(4)

    def wait_w(k):
        sender = lax.rem(f + F - k, F)
        w_copy(0, f, sender).wait_recv()
        w_copy(1, f, sender).wait_recv()

    w_copy(1, f, f).wait_recv()
    loop(1, F, wait_w)

    def part(t):
        if t == 0:
            acc[at(z, TB), :] = dot_t(dh[at(z, TB), :], w2[...])
            return
        for way in range(2):
            rows = at(ring_block(way, t), TB)
            cols = pl.ds(0, CR) if way == 0 else pl.ds(CR, D - CR)
            term = dot_t(dh[rows, cols], w2[:, cols])
            if t < NZ // 2 or (t == NZ // 2 and way == 0):
                acc[rows, :] = term
            else:
                acc[rows, :] += term

    def dconv_copy(block, half):
        rows = pl.ds(pl.multiple_of(half * HALF + block * TB, TB), TB)
        return remote(dcv.at[at(block, TB), :], dch.at[rows, :], x_s.at[block], x_r.at[block], f, pr)

    def dg_copy(n, peer_z, channel):
        return remote(
            dg.at[n, at(peer_z, TB), :], dgt.at[:, at(channel, CB)],
            dg_s.at[n, peer_z], dg_r.at[channel], f, xl * NZ + peer_z,
        )

    own_dg = [
        pltpu.make_async_copy(dg.at[n, at(z, TB), :], dgt.at[:, at(c, CB)], local.at[5 + n])
        for n, c in enumerate((r, pr))
    ]

    def finalize(block):
        rows = at(block, TB)
        for n in range(2):
            d = acc[rows, n * CB : (n + 1) * CB]
            gate = gmn[n, rows, :].astype(F32)
            conv = cmn[n, rows, :].astype(F32)
            gt[n * CB : (n + 1) * CB, rows] = (gate * conv).T.astype(BF)
            dg[n, rows, :] = (d * conv).astype(BF)
            dconv = (d * gate).astype(BF)
            if n == 0:
                dch[pl.ds(pl.multiple_of(xl * HALF + block * TB, TB), TB), :] = dconv
            else:
                dcv[rows, :] = dconv
        dconv_copy(block, xl).start()

    def wait_gate(k):
        sender = lax.rem(z + NZ - k, NZ)
        gate_copy(0, z, sender).wait_recv()
        gate_copy(1, z, sender).wait_recv()

    def step_done(t):
        part(t)
        if t == 0:
            finalize(z)
        elif t == NZ // 2:
            finalize(ring_block(0, t))
        elif t > NZ // 2:
            finalize(ring_block(0, t))
            finalize(ring_block(1, t))

    for t in range(1, min(4, NZ)):
        part(t)
    loop(1, NZ, wait_gate)
    conv_copy.wait_recv()
    step_done(0)
    if NZ <= 4:
        for t in range(NZ // 2, NZ):
            finalize(ring_block(0, t))
            if t > NZ // 2:
                finalize(ring_block(1, t))
    ring(5)
    def send_dg(k):
        peer = lax.rem(z + k, NZ)
        dg_copy(0, peer, r).start()
        dg_copy(1, peer, pr).start()

    for t in range(4, NZ):
        if t == NZ - 1:
            ring(t)
            loop(2, NZ - 1, send_dg)
        step_done(t)
        if t + 2 < NZ - 1:
            ring(t + 2)
    if NZ <= 4:
        loop(2, NZ - 1, send_dg)
    send_dg(1)
    if NZ > 2:
        send_dg(NZ - 1)
    for copy in own_dg:
        copy.start()

    def gw_partial(cols):
        return dot(gt[...], dh[:, at(cols, DB)])

    def gwx_copy(j):
        return remote(gwx.at[j], gwy.at[j], gwx_s.at[j], gwx_r.at[j], twin, r)

    def gwx_step(k):
        j = lax.rem(chip + k, FC)
        gwx[j] = gw_partial(2 * j + 1 - core).astype(BF)
        gwx_copy(j).start()

    loop(0, FC, gwx_step)

    def gwy_copy(h, peer, sender):
        return remote(gws.at[peer, h], gwr.at[sender, h], gw_s.at[h, peer], gw_r.at[h, sender], (xh * NY + peer) * 2 + core, r)

    def gw_step(peer):
        for h in range(NX):
            j = h * NY + peer
            total = gw_partial(2 * j + core)
            gwx_copy(j).wait_recv()
            gws[peer, h] = (total + gwy[j].astype(F32)).astype(BF)

    def gw_send_step(k):
        peer = lax.rem(y + k, NY)
        gw_step(peer)
        for h in range(NX):
            gwy_copy(h, peer, y).start()

    loop(1, NY, gw_send_step)
    gw_step(y)

    loop(0, NZ, lambda k: dconv_copy(k, 1 - xl).wait_recv())
    loop(0, CHUNKS, plane_step(dch), COLS)
    rows_product(dsp, fsp, True, True)

    def dm_copy(peer, sender):
        return remote(dms.at[at(peer, TB), :], dmt.at[:, at(sender, CB)], dm_s.at[peer], dm_r.at[sender], f, peer)

    def dm_send(peer):
        @pl.when(peer != r)
        def _():
            dm_copy(peer, r).start()

    def dmixed_step(k):
        chunk = lax.rem(lax.div(r * TB, CH) + 1 + k, CHUNKS)
        dms[at(chunk, CH), :] = columns_inv(chunk).astype(BF)
        for n in range(CH // TB):
            dm_send(chunk * (CH // TB) + n)

    loop(0, CHUNKS, dmixed_step, COLS)
    own_dm = pltpu.make_async_copy(dms.at[at(r, TB), :], dmt.at[:, at(r, CB)], local.at[7])
    own_dm.start()

    def gwz_copy(h, n):
        return remote(gwp.at[h, n], gwq.at[h, n], gwz_s.at[h, n], gwz_r.at[h, n], (lax.rem(xh + h, NX) * NY + y) * 2 + core, (r, pr)[n])

    def gw_over_y():
        for h in range(NX):
            block = lax.rem(xh + h, NX)
            total = gws[y, block].astype(F32)
            for k in range(1, NY):
                sender = lax.rem(y + k, NY)
                gwy_copy(block, y, sender).wait_recv()
                total = total + gwr[sender, block].astype(F32)
            if h == 0:
                gw_out[...] = total[:CB]
            else:
                gwp[h, 0] = total[:CB].astype(BF)
                gwz_copy(h, 0).start()
            gwp[h, 1] = total[CB:].astype(BF)
            gwz_copy(h, 1).start()

    rows_product(dsp, msp, True, False)

    def gf_step(k):
        gff[at(k, CH), :] = columns_inv(k)

    loop(0, CHUNKS, gf_step, COLS)

    def gfx_copy(j):
        return remote(gfx.at[j], gfy.at[j], gfx_s.at[j], gfx_r.at[j], twin, r)

    def gfx_step(j):
        gfx[j] = gff[at(2 * j + 1 - core, PB), :].astype(BF)
        gfx_copy(j).start()

    loop(0, FC, gfx_step)

    def gf_copy(peer, sender):
        return remote(gfs.at[peer], gfr.at[sender], gf_s.at[peer], gf_r.at[sender], 2 * peer + core, r)

    def gf_sum(j):
        gfx_copy(j).wait_recv()
        gfs[j] = (gff[at(2 * j + core, PB), :] + gfy[j].astype(F32)).astype(BF)

    def gf_send_step(k):
        j = lax.rem(chip + k, FC)
        gf_sum(j)
        gf_copy(j, chip).start()

    loop(1, FC, gf_send_step)
    gf_sum(chip)
    gw_over_y()

    gfr[chip] = gfs[chip]
    loop(1, FC, lambda k: gf_copy(chip, lax.rem(chip + FC - k, FC)).wait_recv())
    total = gfr[0].astype(F32)
    for n in range(1, FC):
        total = total + gfr[n].astype(F32)
    gf_out[...] = total.T * (1.0 / F)

    total = gw_out[...]
    for h in range(NX):
        for n in range(2):
            if h + n > 0:
                gwz_copy(h, n).wait_recv()
                total = total + gwq[h, n].astype(F32)
    gw_out[...] = total * (1.0 / F)

    for copy in own_dg:
        copy.wait()

    def dg_arrive(k):
        sender = lax.rem(z + NZ - k, NZ)
        dg_copy(0, z, xl * NZ + sender).wait_recv()
        dg_copy(1, z, (1 - xl) * NZ + sender).wait_recv()

    loop(1, NZ, dg_arrive)

    own_dm.wait()
    loop(1, R, lambda k: dm_copy(r, lax.rem(r + R - k, R)).wait_recv())

    for step in range(NZ - 1):
        for way in range(2):
            for sub in range(SUB):
                ring_copy(way, sub, step, ring_block(way, step)).wait_send()

    def row_sent(k):
        peer = lax.rem(r + k, R)
        mx_copy(peer, r).wait_send()
        dm_copy(peer, r).wait_send()

    loop(1, R, row_sent)

    def z_sent(k):
        peer = lax.rem(z + k, NZ)
        for n in range(2):
            gate_copy(n, peer, z).wait_send()
            dg_copy(n, peer, (r, pr)[n]).wait_send()

    loop(1, NZ, z_sent)
    loop(0, NZ, lambda k: dconv_copy(k, xl).wait_send())

    def plane_sent(k):
        peer = lax.rem(f + k, F)
        for n in range(2):
            w_copy(n, peer, f).wait_send()

    loop(1, F, plane_sent)

    def chip_sent(k):
        peer = lax.rem(chip + k, FC)
        gf_copy(peer, chip).wait_send()

    loop(1, FC, chip_sent)

    def twin_sent(j):
        gwx_copy(j).wait_send()
        gfx_copy(j).wait_send()

    loop(0, FC, twin_sent)

    def y_sent(k):
        for h in range(NX):
            gwy_copy(h, lax.rem(y + k, NY), y).wait_send()

    loop(1, NY, y_sent)
    for h in range(NX):
        for n in range(2):
            if h + n > 0:
                gwz_copy(h, n).wait_send()
    w_copy(1, f, f).wait_send()
    conv_copy.wait_send()


def finish(parts, proj, dmixed, dgate, gw, gf, out, gw_out, gf_out, factors, d, grads, gw_held, gf_held, load, store):
    TB, D = dmixed.shape
    rows = TB // parts
    loads = []
    for n in range(parts):
        place = pl.ds(n * rows, rows)
        loads.append((
            pltpu.make_async_copy(proj.at[place, pl.ds(0, 2 * D)], factors.at[place, :], load.at[0, n]),
            pltpu.make_async_copy(dmixed.at[place, :], d.at[place, :], load.at[1, n]),
            pltpu.make_async_copy(dgate.at[place, :], grads.at[place, pl.ds(2 * D, D)], load.at[2, n]),
        ))
    loads.append((
        pltpu.make_async_copy(gw, gw_held, load.at[0, parts]),
        pltpu.make_async_copy(gf, gf_held, load.at[1, parts]),
    ))
    for group in loads:
        for copy in group:
            copy.start()
    stores = []
    for n in range(parts):
        place = pl.ds(n * rows, rows)
        for copy in loads[n]:
            copy.wait()
        x = d[place, :].astype(F32)
        grads[place, :D] = (x * factors[place, D:].astype(F32)).astype(BF)
        grads[place, D : 2 * D] = (x * factors[place, :D].astype(F32)).astype(BF)
        stores.append(pltpu.make_async_copy(grads.at[place, :], out.at[place, :], store.at[n]))
        stores[-1].start()
    for copy in loads[parts]:
        copy.wait()
    stores.append(pltpu.make_async_copy(gw_held, gw_out, store.at[parts]))
    stores.append(pltpu.make_async_copy(gf_held, gf_out, store.at[parts + 1]))
    for copy in stores[parts:]:
        copy.start()
    for copy in stores:
        copy.wait()


def local(R, F, proj, dout, filt, w):
    proj, dout = proj.reshape(proj.shape[1:]), dout.reshape(dout.shape[1:])
    D = dout.shape[1]
    NZ = R // 2
    TB, CB, DB, PB = POS // R, D // R, D // F, POS // F
    CR = D * RIGHT // 16 // (128 * SUB) * (128 * SUB)
    NX = 2 if F >= 8 else 1
    NY = F // 2 // NX
    tables = [jnp.asarray(t) for t in build_tables()]
    vmem = pl.BlockSpec(memory_space=pltpu.VMEM)
    hbm = pl.BlockSpec(memory_space=pl.ANY)
    dma = pltpu.SemaphoreType.DMA
    spectrum = pltpu.VMEM((LC + 2, LR, CB), F32)
    grads = pl.pallas_call(
        functools.partial(kernel, R, F, D, CR),
        out_shape=(
            jax.ShapeDtypeStruct((TB, D), BF),
            jax.ShapeDtypeStruct((TB, D), BF),
            jax.ShapeDtypeStruct((CB, DB), F32),
            jax.ShapeDtypeStruct((CB, PB), F32),
        ),
        in_specs=[
            hbm, hbm, hbm, hbm,
        ] + [hbm] * len(tables),
        out_specs=(hbm, hbm, vmem, vmem),
        scratch_shapes=[
            pltpu.VMEM((CB, POS), F32),
        ] + [pltpu.VMEM(t.shape, BF) for t in tables] + [
            pltpu.VMEM((TB, D), BF), pltpu.VMEM((TB, D), BF),
            pltpu.VMEM((TB, D), BF),
            pltpu.VMEM((POS, CB), BF),
            pltpu.VMEM((2, HALF, CB), BF),
            pltpu.VMEM((2, HALF, CB), BF),
            pltpu.VMEM((HALF, CB), BF),
            pltpu.VMEM((HALF, D), BF),
            pltpu.VMEM((2 * CB, D), BF),
            spectrum, spectrum, spectrum,
            pltpu.VMEM((LC, LR, CB), F32),
            pltpu.VMEM((HALF, 2 * CB), F32),
            pltpu.VMEM((2 * CB, HALF), BF),
            pltpu.VMEM((HALF, CB), BF),
            pltpu.VMEM((POS, CB), BF),
            pltpu.VMEM((2, HALF, CB), BF),
            pltpu.VMEM((POS, CB), BF),
            pltpu.VMEM((F // 2, 2 * CB, DB), BF), pltpu.VMEM((F // 2, 2 * CB, DB), BF),
            pltpu.VMEM((NY, NX, 2 * CB, DB), BF), pltpu.VMEM((NY, NX, 2 * CB, DB), BF),
            pltpu.VMEM((NX, 2, CB, DB), BF), pltpu.VMEM((NX, 2, CB, DB), BF),
            pltpu.VMEM((POS, CB), F32),
            pltpu.VMEM((F // 2, PB, CB), BF), pltpu.VMEM((F // 2, PB, CB), BF),
            pltpu.VMEM((F // 2, PB, CB), BF), pltpu.VMEM((F // 2, PB, CB), BF),
            dma((23,)),
            dma((2 * SUB, NZ)), dma((2 * SUB, NZ)),
            dma((R,)), dma((R,)),
            dma((2, NZ)), dma((2, NZ)),
            dma((2, F)), dma((2, F)),
            dma((NZ + 1,)), dma((NZ + 1,)),
            dma((2, NZ)), dma((R,)),
            dma((R,)), dma((R,)),
            dma((F // 2,)), dma((F // 2,)), dma((NX, NY)), dma((NX, NY)),
            dma((NX, 2)), dma((NX, 2)),
            dma((F // 2,)), dma((F // 2,)), dma((F // 2,)), dma((F // 2,)),
        ],
        compiler_params=pltpu.CompilerParams(
            collective_id=0, has_side_effects=True, vmem_limit_bytes=62 * 1024 * 1024
        ),
    )(proj, dout, w, filt, *tables)
    dmixed, dgate, gw, gf = grads
    parts = 4
    grad_proj, gw, gf = pl.pallas_call(
        functools.partial(finish, parts),
        out_shape=(
            jax.ShapeDtypeStruct((TB, 3 * D), BF),
            jax.ShapeDtypeStruct((CB, DB), F32),
            jax.ShapeDtypeStruct((CB, PB), F32),
        ),
        in_specs=[hbm] * 5,
        out_specs=(hbm, hbm, hbm),
        scratch_shapes=[
            pltpu.VMEM((TB, 2 * D), BF),
            pltpu.VMEM((TB, D), BF),
            pltpu.VMEM((TB, 3 * D), BF),
            pltpu.VMEM((CB, DB), F32),
            pltpu.VMEM((CB, PB), F32),
            dma((3, parts + 1)), dma((parts + 2,)),
        ],
        compiler_params=pltpu.CompilerParams(vmem_limit_bytes=62 * 1024 * 1024),
    )(proj, dmixed, dgate, gw, gf)
    return grad_proj[None], gw, gf


def solution(mesh):
    placed = (P("frame", "row", None), P("frame", "row", None), P("row", None), P("row", "frame"))
    return jax.shard_map(
        functools.partial(local, mesh.shape["row"], mesh.shape["frame"]),
        mesh=mesh,
        in_specs=placed,
        out_specs=(P("frame", "row", None), P("row", "frame"), P("row", "frame")),
        check_vma=False,
    )
```

```python
import functools

import jax
import jax.numpy as jnp
import ml_dtypes
import numpy as np
from jax import lax
from jax.experimental import pallas as pl
from jax.experimental.pallas import tpu as pltpu
from jax.sharding import PartitionSpec as P

LR = 64
LC = 32
POS = LR * LC
HALF = POS // 2
RIGHT = 8
SUB = 2
ROWS = 5
COLS = 4
G = 8
MESH = pl.DeviceIdType.MESH
BF = jnp.bfloat16
F32 = jnp.float32


def split_table(table):
    high = table.astype(ml_dtypes.bfloat16)
    low = (table - high.astype(np.float64)).astype(ml_dtypes.bfloat16)
    return high, low


def build_tables():
    j = np.arange(LC)
    fwd = np.zeros((LC, LC))
    inv = np.zeros((LC, LC))
    fwd[0], inv[:, 0] = 1.0, 1.0
    fwd[1] = np.cos(np.pi * j)
    inv[:, 1] = np.cos(np.pi * j)
    for l in range(1, LC // 2):
        angle = 2 * np.pi * ((j * l) % LC) / LC
        fwd[2 * l], fwd[2 * l + 1] = np.cos(angle), -np.sin(angle)
        inv[:, 2 * l], inv[:, 2 * l + 1] = 2 * np.cos(angle), -2 * np.sin(angle)
    inv = inv / POS
    eye = np.eye(G)
    col_fwd = np.einsum("qj,ab->qabj", fwd, eye).reshape(G * LC, G * LC)
    col_inv = np.einsum("jq,ab->ajqb", inv, eye).reshape(G * LC, G * LC)
    i = np.arange(LR)
    angle = 2 * np.pi * ((i[:, None] * i[None, :]) % LR) / LR
    c, s = np.cos(angle), np.sin(angle)
    o = np.zeros_like(c)
    row_fwd = np.block([[c, s], [-s, c]])
    row_inv = np.block([[c, -s], [s, c]])
    edge_fwd = np.block([[c, o], [-s, o], [o, c], [o, -s]])
    edge_inv = np.block([[c, -s, o, o], [o, o, c, -s]])
    out = []
    for table in (col_fwd, row_fwd, edge_fwd, row_inv, edge_inv, col_inv):
        out.extend(split_table(table))
    return tuple(out)


def split(x):
    high = x.astype(BF)
    return high, (x - high.astype(F32)).astype(BF)


def dot(a, b):
    return jnp.dot(a, b, preferred_element_type=F32)


def dot_t(a, b):
    return lax.dot_general(a, b, (((1,), (1,)), ((), ())), preferred_element_type=F32)


def dot3(high, low, x, product=dot):
    x_high, x_low = split(x)
    return product(high, x_high) + product(high, x_low) + product(low, x_high)


def kernel(
    R, F, D, CR,
    proj, dout, w, filt_hbm, t0, t1, t2, t3, t4, t5, t6, t7, t8, t9, t10, t11,
    dmt, dgt, gw_hbm, gf_hbm,
    gw_out, gf_out, filt, a1h, a1l, a2h, a2l, azh, azl, b2h, b2l, bzh, bzl, b1h, b1l,
    value, gate_a, mx, mch, gmn, cmn, cvo, dh, w2, fsp, msp, dsp, tmp, acc, gt, dcv, dch, dg, dms,
    gwx, gwy, gws, gwr, gwp, gwq, gff, gfx, gfy, gfs, gfr,
    local, ring_s, ring_r, mx_s, mx_r, gate_s, gate_r, w_s, w_r, x_s, x_r, dg_s, dg_r, dm_s, dm_r,
    gwx_s, gwx_r, gw_s, gw_r, gwz_s, gwz_r, gfx_s, gfx_r, gf_s, gf_r,
):
    NZ = R // 2
    TB, CB, DB, PB = POS // R, D // R, D // F, POS // F
    f, r = lax.axis_index("frame"), lax.axis_index("row")
    xl, z = lax.div(r, NZ), lax.rem(r, NZ)
    pr = (1 - xl) * NZ + z
    right = xl * NZ + lax.rem(z + 1, NZ)
    left = xl * NZ + lax.rem(z + NZ - 1, NZ)
    FC = F // 2
    chip, core = lax.div(f, 2), lax.rem(f, 2)
    twin = f + 1 - 2 * core
    NX = 2 if F >= 8 else 1
    NY = FC // NX
    xh, y = lax.div(chip, NY), lax.rem(chip, NY)

    def at(index, size):
        return pl.ds(pl.multiple_of(index * size, size), size)

    def remote(src, dst, send, recv, frame, row):
        return pltpu.make_async_remote_copy(
            src_ref=src, dst_ref=dst, send_sem=send, recv_sem=recv,
            device_id={"frame": frame, "row": row}, device_id_type=MESH,
        )

    def loop(start, stop, step, unroll=1):
        def body(k, carry):
            step(k)
            return carry

        lax.fori_loop(start, stop, body, 0, unroll=unroll)

    barrier = pltpu.get_barrier_semaphore()

    def greet(frame, row):
        pl.semaphore_signal(barrier, inc=1, device_id={"frame": frame, "row": row}, device_id_type=MESH)

    loop(1, R, lambda k: greet(f, lax.rem(r + k, R)))

    def greet_plane(k):
        greet(lax.rem(f + k, F), r)
        greet(lax.rem(f + k, F), pr)

    loop(1, F, greet_plane)

    own_dout = pltpu.make_async_copy(dout, dh.at[at(z, TB), :], local.at[0])
    own_w = pltpu.make_async_copy(w, w2.at[pl.ds(0, CB), at(f, DB)], local.at[1])
    own_gate = [
        pltpu.make_async_copy(proj.at[:, at(2 * R + c, CB)], gmn.at[n, at(z, TB), :], local.at[2 + n])
        for n, c in enumerate((r, pr))
    ]
    own_value = pltpu.make_async_copy(proj.at[:, pl.ds(0, D)], value, local.at[8])
    own_a = pltpu.make_async_copy(proj.at[:, pl.ds(D, D)], gate_a, local.at[9])
    own_value.start()
    own_a.start()
    own_dout.start()
    own_w.start()
    for copy in own_gate:
        copy.start()
    own_tables = [
        pltpu.make_async_copy(pair[0], pair[1], local.at[10 + n])
        for n, pair in enumerate(
            zip(
                (filt_hbm, t0, t1, t2, t3, t4, t5, t6, t7, t8, t9, t10, t11),
                (filt, a1h, a1l, a2h, a2l, azh, azl, b2h, b2l, bzh, bzl, b1h, b1l),
            )
        )
    ]
    for copy in own_tables:
        copy.start()

    own_value.wait()
    own_a.wait()
    mx[...] = (value[...].astype(F32) * gate_a[...].astype(F32)).astype(BF)
    own_mx = pltpu.make_async_copy(mx.at[:, at(r, CB)], mch.at[at(r, TB), :], local.at[4])
    own_mx.start()
    pl.semaphore_wait(barrier, (R - 1) + 2 * (F - 1))

    def ring_part(way, sub):
        width = (CR if way == 0 else D - CR) // SUB
        return pl.ds((0 if way == 0 else CR) + sub * width, width)

    def ring_copy(way, sub, step, block):
        place = dh.at[at(block, TB), ring_part(way, sub)]
        n = way * SUB + sub
        first = dout.at[:, ring_part(way, sub)] if step == 0 else place
        return remote(first, place, ring_s.at[n, step], ring_r.at[n, step], f, (right, left)[way])

    def ring_block(way, step):
        return lax.rem(z + NZ - step, NZ) if way == 0 else lax.rem(z + step, NZ)

    def ring(step):
        if step < NZ:
            for sub in range(SUB):
                for way in range(2):
                    if step > 0:
                        ring_copy(way, sub, step - 1, ring_block(way, step)).wait_recv()
                    if step < NZ - 1:
                        ring_copy(way, sub, step, ring_block(way, step)).start()

    def mx_copy(peer, sender):
        return remote(mx.at[:, at(peer, CB)], mch.at[at(sender, TB), :], mx_s.at[peer], mx_r.at[sender], f, peer)

    def gate_copy(n, peer_z, sender_z):
        c = (xl if n == 0 else 1 - xl) * NZ + peer_z
        return remote(
            proj.at[:, at(2 * R + c, CB)], gmn.at[n, at(sender_z, TB), :],
            gate_s.at[n, peer_z], gate_r.at[n, sender_z], f, xl * NZ + peer_z,
        )

    def w_copy(n, peer, sender):
        return remote(
            w, w2.at[pl.ds(n * CB, CB), at(sender, DB)], w_s.at[n, peer], w_r.at[n, sender], peer, (r, pr)[n]
        )

    def send_w(k):
        peer = lax.rem(f + k, F)
        w_copy(0, peer, f).start()
        w_copy(1, peer, f).start()

    ring(0)

    def send_mx(k):
        peer = lax.rem(r + k, R)
        mx_copy(peer, r).start()

    loop(1, R, send_mx)

    def send_gate(k):
        peer = lax.rem(z + k, NZ)
        gate_copy(0, peer, z).start()
        gate_copy(1, peer, z).start()

    loop(1, NZ, send_gate)
    w_copy(1, f, f).start()
    loop(1, F, send_w)

    def columns(k, part):
        tmp[:, at(k, G), :] = part.reshape(LC, G, CB)

    def pair(ref, index):
        return ref[pl.ds(index, 2)].reshape(2 * LR, CB)

    def rows_fwd(dst):
        edge = dot3(azh[...], azl[...], pair(tmp, 0)).reshape(4, LR, CB)
        dst[0:2] = edge[0:2]
        dst[LC : LC + 2] = edge[2:4]

        def step(l):
            dst[pl.ds(2 * l, 2)] = dot3(a2h[...], a2l[...], pair(tmp, 2 * l)).reshape(2, LR, CB)

        loop(1, LC // 2, step, ROWS)

    def multiply(a, b, conjugate):
        are, aim, bre, bim = a[0], a[1], b[0], b[1]
        if conjugate:
            both = are * bre + aim * bim, aim * bre - are * bim
        else:
            both = are * bre - aim * bim, are * bim + aim * bre
        return jnp.concatenate(both, axis=0)

    def rows_product(a, b, conjugate, forward):
        if forward:
            edge = dot3(azh[...], azl[...], pair(tmp, 0)).reshape(4, LR, CB)
            a[0:2] = edge[0:2]
            a[LC : LC + 2] = edge[2:4]
        else:
            edge = jnp.concatenate((a[0:2], a[LC : LC + 2]), axis=0)
        edge = jnp.concatenate((multiply(edge[0:2], b[0:2], conjugate), multiply(edge[2:4], b[LC : LC + 2], conjugate)), axis=0)
        tmp[0:2] = dot3(bzh[...], bzl[...], edge).reshape(2, LR, CB)

        def step(l):
            place = pl.ds(2 * l, 2)
            if forward:
                spectrum = dot3(a2h[...], a2l[...], pair(tmp, 2 * l)).reshape(2, LR, CB)
                a[place] = spectrum
            else:
                spectrum = a[place]
            tmp[place] = dot3(b2h[...], b2l[...], multiply(spectrum, b[place], conjugate)).reshape(2, LR, CB)

        loop(1, LC // 2, step, ROWS)

    def columns_inv(k):
        return dot3(b1h[...], b1l[...], tmp[:, at(k, G), :].reshape(G * LC, CB))

    CH = G * LC
    CHUNKS = POS // CH

    def filt_step(k):
        columns(k, dot3(a1h[...], a1l[...], filt[:, at(k, CH)], dot_t))

    for copy in own_tables:
        copy.wait()
    loop(0, CHUNKS, filt_step, COLS)
    ring(1)
    rows_fwd(fsp)

    own_mx.wait()

    def wait_mx(k):
        sender = lax.rem(r + R - k, R)
        mx_copy(r, sender).wait_recv()

    loop(1, R, wait_mx)
    ring(2)

    def plane_step(src):
        def step(k):
            x = src[at(k, CH), :]
            columns(k, dot(a1h[...], x) + dot(a1l[...], x))

        return step

    loop(0, CHUNKS, plane_step(mch), COLS)
    ring(3)
    rows_product(msp, fsp, False, True)

    def conv_step(k):
        cmn[0, at(k, CH), :] = columns_inv(xl * (CHUNKS // 2) + k).astype(BF)
        cvo[at(k, CH), :] = columns_inv((1 - xl) * (CHUNKS // 2) + k).astype(BF)

    loop(0, CHUNKS // 2, conv_step, COLS // 2)
    conv_copy = remote(cvo, cmn.at[1], x_s.at[NZ], x_r.at[NZ], f, pr)
    conv_copy.start()
    for copy in own_gate:
        copy.wait()
    own_w.wait()
    own_dout.wait()
    ring(4)

    def wait_w(k):
        sender = lax.rem(f + F - k, F)
        w_copy(0, f, sender).wait_recv()
        w_copy(1, f, sender).wait_recv()

    w_copy(1, f, f).wait_recv()
    loop(1, F, wait_w)

    def part(t):
        if t == 0:
            acc[at(z, TB), :] = dot_t(dh[at(z, TB), :], w2[...])
            return
        for way in range(2):
            rows = at(ring_block(way, t), TB)
            cols = pl.ds(0, CR) if way == 0 else pl.ds(CR, D - CR)
            term = dot_t(dh[rows, cols], w2[:, cols])
            if t < NZ // 2 or (t == NZ // 2 and way == 0):
                acc[rows, :] = term
            else:
                acc[rows, :] += term

    def dconv_copy(block, half):
        rows = pl.ds(pl.multiple_of(half * HALF + block * TB, TB), TB)
        return remote(dcv.at[at(block, TB), :], dch.at[rows, :], x_s.at[block], x_r.at[block], f, pr)

    def dg_copy(n, peer_z, channel):
        return remote(
            dg.at[n, at(peer_z, TB), :], dgt.at[:, at(channel, CB)],
            dg_s.at[n, peer_z], dg_r.at[channel], f, xl * NZ + peer_z,
        )

    own_dg = [
        pltpu.make_async_copy(dg.at[n, at(z, TB), :], dgt.at[:, at(c, CB)], local.at[5 + n])
        for n, c in enumerate((r, pr))
    ]

    def finalize(block):
        rows = at(block, TB)
        for n in range(2):
            d = acc[rows, n * CB : (n + 1) * CB]
            gate = gmn[n, rows, :].astype(F32)
            conv = cmn[n, rows, :].astype(F32)
            gt[n * CB : (n + 1) * CB, rows] = (gate * conv).T.astype(BF)
            dg[n, rows, :] = (d * conv).astype(BF)
            dconv = (d * gate).astype(BF)
            if n == 0:
                dch[pl.ds(pl.multiple_of(xl * HALF + block * TB, TB), TB), :] = dconv
            else:
                dcv[rows, :] = dconv
        dconv_copy(block, xl).start()

    def wait_gate(k):
        sender = lax.rem(z + NZ - k, NZ)
        gate_copy(0, z, sender).wait_recv()
        gate_copy(1, z, sender).wait_recv()

    def step_done(t):
        part(t)
        if t == 0:
            finalize(z)
        elif t == NZ // 2:
            finalize(ring_block(0, t))
        elif t > NZ // 2:
            finalize(ring_block(0, t))
            finalize(ring_block(1, t))

    for t in range(1, min(4, NZ)):
        part(t)
    loop(1, NZ, wait_gate)
    conv_copy.wait_recv()
    step_done(0)
    if NZ <= 4:
        for t in range(NZ // 2, NZ):
            finalize(ring_block(0, t))
            if t > NZ // 2:
                finalize(ring_block(1, t))
    ring(5)
    def send_dg(k):
        peer = lax.rem(z + k, NZ)
        dg_copy(0, peer, r).start()
        dg_copy(1, peer, pr).start()

    for t in range(4, NZ):
        if t == NZ - 1:
            ring(t)
            loop(2, NZ - 1, send_dg)
        step_done(t)
        if t + 2 < NZ - 1:
            ring(t + 2)
    if NZ <= 4:
        loop(2, NZ - 1, send_dg)
    send_dg(1)
    if NZ > 2:
        send_dg(NZ - 1)
    for copy in own_dg:
        copy.start()

    def gw_partial(cols):
        return dot(gt[...], dh[:, at(cols, DB)])

    def gwx_copy(j):
        return remote(gwx.at[j], gwy.at[j], gwx_s.at[j], gwx_r.at[j], twin, r)

    def gwx_step(k):
        j = lax.rem(chip + k, FC)
        gwx[j] = gw_partial(2 * j + 1 - core).astype(BF)
        gwx_copy(j).start()

    loop(0, FC, gwx_step)

    def gwy_copy(h, peer, sender):
        return remote(gws.at[peer, h], gwr.at[sender, h], gw_s.at[h, peer], gw_r.at[h, sender], (xh * NY + peer) * 2 + core, r)

    def gw_step(peer):
        for h in range(NX):
            j = h * NY + peer
            total = gw_partial(2 * j + core)
            gwx_copy(j).wait_recv()
            gws[peer, h] = (total + gwy[j].astype(F32)).astype(BF)

    def gw_send_step(k):
        peer = lax.rem(y + k, NY)
        gw_step(peer)
        for h in range(NX):
            gwy_copy(h, peer, y).start()

    loop(1, NY, gw_send_step)
    gw_step(y)

    loop(0, NZ, lambda k: dconv_copy(k, 1 - xl).wait_recv())
    loop(0, CHUNKS, plane_step(dch), COLS)
    rows_product(dsp, fsp, True, True)

    def dm_copy(peer, sender):
        return remote(dms.at[at(peer, TB), :], dmt.at[:, at(sender, CB)], dm_s.at[peer], dm_r.at[sender], f, peer)

    def dm_send(peer):
        @pl.when(peer != r)
        def _():
            dm_copy(peer, r).start()

    def dmixed_step(k):
        chunk = lax.rem(lax.div(r * TB, CH) + 1 + k, CHUNKS)
        dms[at(chunk, CH), :] = columns_inv(chunk).astype(BF)
        for n in range(CH // TB):
            dm_send(chunk * (CH // TB) + n)

    loop(0, CHUNKS, dmixed_step, COLS)
    own_dm = pltpu.make_async_copy(dms.at[at(r, TB), :], dmt.at[:, at(r, CB)], local.at[7])
    own_dm.start()

    def gwz_copy(h, n):
        return remote(gwp.at[h, n], gwq.at[h, n], gwz_s.at[h, n], gwz_r.at[h, n], (lax.rem(xh + h, NX) * NY + y) * 2 + core, (r, pr)[n])

    def gw_over_y():
        for h in range(NX):
            block = lax.rem(xh + h, NX)
            total = gws[y, block].astype(F32)
            for k in range(1, NY):
                sender = lax.rem(y + k, NY)
                gwy_copy(block, y, sender).wait_recv()
                total = total + gwr[sender, block].astype(F32)
            if h == 0:
                gw_out[...] = total[:CB]
            else:
                gwp[h, 0] = total[:CB].astype(BF)
                gwz_copy(h, 0).start()
            gwp[h, 1] = total[CB:].astype(BF)
            gwz_copy(h, 1).start()

    rows_product(dsp, msp, True, False)

    def gf_step(k):
        gff[at(k, CH), :] = columns_inv(k)

    loop(0, CHUNKS, gf_step, COLS)

    def gfx_copy(j):
        return remote(gfx.at[j], gfy.at[j], gfx_s.at[j], gfx_r.at[j], twin, r)

    def gfx_step(j):
        gfx[j] = gff[at(2 * j + 1 - core, PB), :].astype(BF)
        gfx_copy(j).start()

    loop(0, FC, gfx_step)

    def gf_copy(peer, sender):
        return remote(gfs.at[peer], gfr.at[sender], gf_s.at[peer], gf_r.at[sender], 2 * peer + core, r)

    def gf_sum(j):
        gfx_copy(j).wait_recv()
        gfs[j] = (gff[at(2 * j + core, PB), :] + gfy[j].astype(F32)).astype(BF)

    def gf_send_step(k):
        j = lax.rem(chip + k, FC)
        gf_sum(j)
        gf_copy(j, chip).start()

    loop(1, FC, gf_send_step)
    gf_sum(chip)
    gw_over_y()

    gfr[chip] = gfs[chip]
    loop(1, FC, lambda k: gf_copy(chip, lax.rem(chip + FC - k, FC)).wait_recv())
    total = gfr[0].astype(F32)
    for n in range(1, FC):
        total = total + gfr[n].astype(F32)
    gf_out[...] = total.T * (1.0 / F)

    total = gw_out[...]
    for h in range(NX):
        for n in range(2):
            if h + n > 0:
                gwz_copy(h, n).wait_recv()
                total = total + gwq[h, n].astype(F32)
    gw_out[...] = total * (1.0 / F)
    sums_out = [
        pltpu.make_async_copy(gw_out, gw_hbm, local.at[23]),
        pltpu.make_async_copy(gf_out, gf_hbm, local.at[24]),
    ]
    for copy in sums_out:
        copy.start()

    for copy in own_dg:
        copy.wait()

    def dg_arrive(k):
        sender = lax.rem(z + NZ - k, NZ)
        dg_copy(0, z, xl * NZ + sender).wait_recv()
        dg_copy(1, z, (1 - xl) * NZ + sender).wait_recv()

    loop(1, NZ, dg_arrive)

    for copy in sums_out:
        copy.wait()
    own_dm.wait()
    loop(1, R, lambda k: dm_copy(r, lax.rem(r + R - k, R)).wait_recv())

    for step in range(NZ - 1):
        for way in range(2):
            for sub in range(SUB):
                ring_copy(way, sub, step, ring_block(way, step)).wait_send()

    def row_sent(k):
        peer = lax.rem(r + k, R)
        mx_copy(peer, r).wait_send()
        dm_copy(peer, r).wait_send()

    loop(1, R, row_sent)

    def z_sent(k):
        peer = lax.rem(z + k, NZ)
        for n in range(2):
            gate_copy(n, peer, z).wait_send()
            dg_copy(n, peer, (r, pr)[n]).wait_send()

    loop(1, NZ, z_sent)
    loop(0, NZ, lambda k: dconv_copy(k, xl).wait_send())

    def plane_sent(k):
        peer = lax.rem(f + k, F)
        for n in range(2):
            w_copy(n, peer, f).wait_send()

    loop(1, F, plane_sent)

    def chip_sent(k):
        peer = lax.rem(chip + k, FC)
        gf_copy(peer, chip).wait_send()

    loop(1, FC, chip_sent)

    def twin_sent(j):
        gwx_copy(j).wait_send()
        gfx_copy(j).wait_send()

    loop(0, FC, twin_sent)

    def y_sent(k):
        for h in range(NX):
            gwy_copy(h, lax.rem(y + k, NY), y).wait_send()

    loop(1, NY, y_sent)
    for h in range(NX):
        for n in range(2):
            if h + n > 0:
                gwz_copy(h, n).wait_send()
    w_copy(1, f, f).wait_send()
    conv_copy.wait_send()


def finish(parts, proj, dmixed, dgate, gw, gf, out, gw_out, gf_out, factors, d, grads, gw_held, gf_held, load, store):
    TB, D = dmixed.shape
    rows = TB // parts
    loads = []
    for n in range(parts):
        place = pl.ds(n * rows, rows)
        loads.append((
            pltpu.make_async_copy(proj.at[place, pl.ds(0, 2 * D)], factors.at[place, :], load.at[0, n]),
            pltpu.make_async_copy(dmixed.at[place, :], d.at[place, :], load.at[1, n]),
            pltpu.make_async_copy(dgate.at[place, :], grads.at[place, pl.ds(2 * D, D)], load.at[2, n]),
        ))
    loads.append((
        pltpu.make_async_copy(gw, gw_held, load.at[0, parts]),
        pltpu.make_async_copy(gf, gf_held, load.at[1, parts]),
    ))
    for group in loads:
        for copy in group:
            copy.start()
    stores = []
    for n in range(parts):
        place = pl.ds(n * rows, rows)
        for copy in loads[n]:
            copy.wait()
        x = d[place, :].astype(F32)
        grads[place, :D] = (x * factors[place, D:].astype(F32)).astype(BF)
        grads[place, D : 2 * D] = (x * factors[place, :D].astype(F32)).astype(BF)
        stores.append(pltpu.make_async_copy(grads.at[place, :], out.at[place, :], store.at[n]))
        stores[-1].start()
    for copy in loads[parts]:
        copy.wait()
    stores.append(pltpu.make_async_copy(gw_held, gw_out, store.at[parts]))
    stores.append(pltpu.make_async_copy(gf_held, gf_out, store.at[parts + 1]))
    for copy in stores[parts:]:
        copy.start()
    for copy in stores:
        copy.wait()


def local(R, F, proj, dout, filt, w):
    proj, dout = proj.reshape(proj.shape[1:]), dout.reshape(dout.shape[1:])
    D = dout.shape[1]
    NZ = R // 2
    TB, CB, DB, PB = POS // R, D // R, D // F, POS // F
    CR = D * RIGHT // 16 // (128 * SUB) * (128 * SUB)
    NX = 2 if F >= 8 else 1
    NY = F // 2 // NX
    tables = [jnp.asarray(t) for t in build_tables()]
    hbm = pl.BlockSpec(memory_space=pl.ANY)
    dma = pltpu.SemaphoreType.DMA
    spectrum = pltpu.VMEM((LC + 2, LR, CB), F32)
    grads = pl.pallas_call(
        functools.partial(kernel, R, F, D, CR),
        out_shape=(
            jax.ShapeDtypeStruct((TB, D), BF),
            jax.ShapeDtypeStruct((TB, D), BF),
            jax.ShapeDtypeStruct((CB, DB), F32),
            jax.ShapeDtypeStruct((CB, PB), F32),
        ),
        in_specs=[
            hbm, hbm, hbm, hbm,
        ] + [hbm] * len(tables),
        out_specs=(hbm, hbm, hbm, hbm),
        scratch_shapes=[
            pltpu.VMEM((CB, DB), F32), pltpu.VMEM((CB, PB), F32),
            pltpu.VMEM((CB, POS), F32),
        ] + [pltpu.VMEM(t.shape, BF) for t in tables] + [
            pltpu.VMEM((TB, D), BF), pltpu.VMEM((TB, D), BF),
            pltpu.VMEM((TB, D), BF),
            pltpu.VMEM((POS, CB), BF),
            pltpu.VMEM((2, HALF, CB), BF),
            pltpu.VMEM((2, HALF, CB), BF),
            pltpu.VMEM((HALF, CB), BF),
            pltpu.VMEM((HALF, D), BF),
            pltpu.VMEM((2 * CB, D), BF),
            spectrum, spectrum, spectrum,
            pltpu.VMEM((LC, LR, CB), F32),
            pltpu.VMEM((HALF, 2 * CB), F32),
            pltpu.VMEM((2 * CB, HALF), BF),
            pltpu.VMEM((HALF, CB), BF),
            pltpu.VMEM((POS, CB), BF),
            pltpu.VMEM((2, HALF, CB), BF),
            pltpu.VMEM((POS, CB), BF),
            pltpu.VMEM((F // 2, 2 * CB, DB), BF), pltpu.VMEM((F // 2, 2 * CB, DB), BF),
            pltpu.VMEM((NY, NX, 2 * CB, DB), BF), pltpu.VMEM((NY, NX, 2 * CB, DB), BF),
            pltpu.VMEM((NX, 2, CB, DB), BF), pltpu.VMEM((NX, 2, CB, DB), BF),
            pltpu.VMEM((POS, CB), F32),
            pltpu.VMEM((F // 2, PB, CB), BF), pltpu.VMEM((F // 2, PB, CB), BF),
            pltpu.VMEM((F // 2, PB, CB), BF), pltpu.VMEM((F // 2, PB, CB), BF),
            dma((25,)),
            dma((2 * SUB, NZ)), dma((2 * SUB, NZ)),
            dma((R,)), dma((R,)),
            dma((2, NZ)), dma((2, NZ)),
            dma((2, F)), dma((2, F)),
            dma((NZ + 1,)), dma((NZ + 1,)),
            dma((2, NZ)), dma((R,)),
            dma((R,)), dma((R,)),
            dma((F // 2,)), dma((F // 2,)), dma((NX, NY)), dma((NX, NY)),
            dma((NX, 2)), dma((NX, 2)),
            dma((F // 2,)), dma((F // 2,)), dma((F // 2,)), dma((F // 2,)),
        ],
        compiler_params=pltpu.CompilerParams(
            collective_id=0, has_side_effects=True, vmem_limit_bytes=62 * 1024 * 1024
        ),
    )(proj, dout, w, filt, *tables)
    dmixed, dgate, gw, gf = grads
    parts = 2
    grad_proj, gw, gf = pl.pallas_call(
        functools.partial(finish, parts),
        out_shape=(
            jax.ShapeDtypeStruct((TB, 3 * D), BF),
            jax.ShapeDtypeStruct((CB, DB), F32),
            jax.ShapeDtypeStruct((CB, PB), F32),
        ),
        in_specs=[hbm] * 5,
        out_specs=(hbm, hbm, hbm),
        scratch_shapes=[
            pltpu.VMEM((TB, 2 * D), BF),
            pltpu.VMEM((TB, D), BF),
            pltpu.VMEM((TB, 3 * D), BF),
            pltpu.VMEM((CB, DB), F32),
            pltpu.VMEM((CB, PB), F32),
            dma((3, parts + 1)), dma((parts + 2,)),
        ],
        compiler_params=pltpu.CompilerParams(vmem_limit_bytes=62 * 1024 * 1024),
    )(proj, dmixed, dgate, gw, gf)
    return grad_proj[None], gw, gf


def solution(mesh):
    placed = (P("frame", "row", None), P("frame", "row", None), P("row", None), P("row", "frame"))
    return jax.shard_map(
        functools.partial(local, mesh.shape["row"], mesh.shape["frame"]),
        mesh=mesh,
        in_specs=placed,
        out_specs=(P("frame", "row", None), P("row", "frame"), P("row", "frame")),
        check_vma=False,
    )
```
